32 devices in a mesh: lat: 4 (over x, core), lon: 8 (over z, y).
Axes of the slice: x: 2, y: 2, z: 4, core: 2. Of those that a mesh axis runs over, the one named last changes fastest.
Arguments:
- obs_value: float32 [32, 21, 32, 128], P(('lat', 'lon')), may hold values from -6 to 6
- obs_cell: int32 [32, 32, 128], P(('lat', 'lon')), may hold values from 0 to 12287
- obs_count: int32 [32, 32], P(('lat', 'lon')), may hold values from 0 to 128, as said below
- bottom_level: int32 [192, 2048], P('lat', 'lon'), may hold values from 0 to 10
- diffusivity: float32 [2, 192, 2048], P(None, 'lat', 'lon'), may hold values from 0.5 to 16
- partner: int32 [2048], P('lon'), may hold values from 0 to 2047, as said below
- length_scale: float32 [21], replicated, may hold values from 0.25 to 2
- sigma: float32 [21], replicated, may hold values from 0.5 to 2
Outputs:
- obs_fit: float32 [32, 21, 32, 128], P(('lat', 'lon'))
- diffused: float32 [21, 192, 2048], P(None, 'lat', 'lon')
The draws below stay inside these ranges and needn't reach their ends.
Inputs may be any that keep to these rules, and one draw needn't show every extreme that they name: `obs_count`: at most 128 live slots from one device to one owner; in every draw one owner receives 128 from every device. partner[i] = (centre - i) mod 2048 for one centre of each draw.
All inputs are finite; a program needn't handle non-finite values.
Results may differ from the reference program's by a relative error of at most 0.00002.
Values sent between devices are 32-bit elements; how exact they have to be, the bound alone decides.
No kernel may reach another device: no remote copies, remote signals or barrier semaphores. Data moves between devices by JAX's collectives and lax.ppermute only.
A program may use at most 128 MiB of HBM per device.

```python
import math
import jax
import jax.numpy as jnp

LEV = 10
STEPS = 2
SWEEPS = 6
CLAT = 48
CLON = 256
CAP = 128
C = 21
NLAT = 192
NLON = 2048
N_LON = 8
DEVICES = 32


def draw_obs_count(key, part):
    key_dense, key_raw, key_full = jax.random.split(key, 3)
    density = jax.random.randint(key_dense, (DEVICES,), 1, 9)
    ceiling = CAP * density[None, :] // 4 + 1
    raw_counts = jax.random.randint(key_raw, (DEVICES, DEVICES), 0, ceiling)
    counts = jnp.minimum(raw_counts, CAP)
    full_owner = jax.random.randint(key_full, (), 0, DEVICES)
    owners = jnp.arange(DEVICES, dtype=jnp.int32)[None, :]
    return jnp.where(owners == full_owner, CAP, counts).astype(jnp.int32)


def draw_partner(key, part):
    centre = jax.random.randint(key, (), 0, NLON)
    return jnp.mod(centre - jnp.arange(NLON, dtype=jnp.int32), NLON).astype(jnp.int32)


def place_ends(array, rng, least, largest):
    place = [jax.random.randint(jax.random.fold_in(rng, axis), (), 0, length) for axis, length in enumerate(array.shape)]
    widest = array.shape.index(max(array.shape))
    beside = place[:widest] + [(place[widest] + 1) % array.shape[widest]] + place[widest + 1:]
    return array.at[tuple(place)].set(least).at[tuple(beside)].set(largest)


def levels(rng, extent, pieces, least, high):
    loudness = 1.0
    for position, parts in pieces:
        steps = jax.random.uniform(jax.random.fold_in(jax.random.fold_in(rng, 6), position), (parts,), jnp.float32, least / len(pieces), high / len(pieces))
        loudness = loudness * jnp.repeat(jnp.exp(steps), extent[position] // parts).reshape((-1,) + (1,) * (len(extent) - 1 - position))
    return loudness


def gaussian(key, shape, deviation, limit, shards=(), kind=jnp.bfloat16):
    values = jax.random.normal(key, shape, jnp.float32) * deviation
    if len(shards) > 0:
        values = levels(key, shape, shards, -0.22, 0.18) * values
    return jnp.clip(values, min=-limit, max=limit).astype(kind)


def setup_inputs(seed: int = 0) -> dict:
    arg_keys = jax.random.split(jax.random.key(seed), 9)
    obs_value = gaussian(arg_keys[0], (DEVICES, C, DEVICES, CAP), 1.0, 6.0, ((0, 32),), jnp.float32)
    obs_cell = place_ends(jax.random.randint(arg_keys[1], (DEVICES, DEVICES, CAP), 0, CLAT * CLON), jax.random.fold_in(arg_keys[1], 1), 0, (CLAT * CLON) - 1).astype(jnp.int32)
    obs_count = draw_obs_count(jax.random.fold_in(arg_keys[8], 71), 0)
    bottom_level = place_ends(jax.random.randint(arg_keys[3], (NLAT, NLON), 0, LEV + 1), jax.random.fold_in(arg_keys[3], 1), 0, LEV).astype(jnp.int32)
    diffusivity = jnp.clip(jnp.exp(math.log(16.0) - 3.465736 * jax.random.uniform(arg_keys[4], (2, NLAT, NLON), jnp.float32) ** levels(arg_keys[4], (2, NLAT, NLON), ((1, 4), (2, 8)), -0.2, 0.2)), 0.5, 16.0)
    partner = draw_partner(jax.random.fold_in(arg_keys[8], 71), 0)
    length_scale = jnp.clip(jnp.exp(jax.random.uniform(arg_keys[6], (C,), jnp.float32, math.log(0.25), math.log(2.0))), 0.25, 2.0)
    sigma = jnp.clip(jnp.exp(jax.random.uniform(arg_keys[7], (C,), jnp.float32, math.log(0.5), math.log(2.0))), 0.5, 2.0)
    return dict(obs_value=obs_value, obs_cell=obs_cell, obs_count=obs_count, bottom_level=bottom_level, diffusivity=diffusivity, partner=partner, length_scale=length_scale, sigma=sigma)


def level_table():
    return jnp.concatenate([jnp.arange(LEV, dtype=jnp.int32), jnp.arange(LEV, dtype=jnp.int32), jnp.zeros((1,), jnp.int32)])


def neighbours(block, partner):
    east = jnp.roll(block, -1, axis=2)
    west = jnp.roll(block, 1, axis=2)
    north = jnp.concatenate([block[:, 1:], block[:, -1:][:, :, partner]], axis=1)
    south = jnp.concatenate([jnp.zeros_like(block[:, :1]), block[:, :-1]], axis=1)
    return east, west, north, south


def reference(obs_value, obs_cell, obs_count, bottom_level, diffusivity, partner, length_scale, sigma):
    channels = 2 * LEV + 1
    wet_mask = (level_table()[:, None, None] < bottom_level[None]).astype(jnp.float32)
    live_slots = (jnp.arange(CAP, dtype=jnp.int32)[None, None, :] < obs_count[:, :, None]).astype(jnp.float32)
    values = obs_value * live_slots[:, None, :, :]
    owners = jnp.arange(DEVICES, dtype=jnp.int32)
    first_row = (owners // N_LON) * CLAT
    first_col = (owners % N_LON) * CLON
    rows_global = first_row[None, :, None] + obs_cell // CLON
    cols_global = first_col[None, :, None] + obs_cell % CLON
    flat_cells = (rows_global * NLON + cols_global).reshape(-1).astype(jnp.int32)
    spread = jnp.transpose(values, (1, 0, 2, 3)).reshape(channels, -1)
    field = jnp.zeros((channels, NLAT * NLON), jnp.float32).at[:, flat_cells].add(spread)
    field = field.reshape(channels, NLAT, NLON) * (sigma[:, None, None] * wet_mask)
    scale = length_scale[:, None, None]
    wet_e, wet_w, wet_n, wet_s = neighbours(wet_mask, partner)
    lon_e, lon_w, unused_n, unused_s = neighbours(diffusivity[0][None], partner)
    unused_e, unused_w, lat_n, lat_s = neighbours(diffusivity[1][None], partner)
    kappa_lon = diffusivity[0][None]
    kappa_lat = diffusivity[1][None]
    w_east = scale * (0.5 * (kappa_lon + lon_e)) * wet_mask * wet_e
    w_west = scale * (0.5 * (kappa_lon + lon_w)) * wet_mask * wet_w
    w_north = scale * (0.5 * (kappa_lat + lat_n)) * wet_mask * wet_n
    w_south = scale * (0.5 * (kappa_lat + lat_s)) * wet_mask * wet_s
    diagonal_sum = 1.0 + w_east + w_west + w_north + w_south
    state = field
    for step_index in range(STEPS):
        source = state
        for sweep_index in range(SWEEPS):
            east, west, north, south = neighbours(state, partner)
            state = (source + w_east * east + w_west * west + w_north * north + w_south * south) / diagonal_sum
    diffused = sigma[:, None, None] * state
    fits = diffused.reshape(channels, -1)[:, flat_cells].reshape(channels, DEVICES, DEVICES, CAP)
    obs_fit = jnp.transpose(fits, (1, 0, 2, 3)) * live_slots[:, None, :, :]
    return obs_fit, diffused
```

```python
import functools

import jax
import jax.numpy as jnp
from jax import lax
from jax.experimental import pallas as pl
from jax.experimental.pallas import tpu as pltpu
from jax.sharding import PartitionSpec as P

LEV = 10
STEPS = 2
SWEEPS = 6
DEPTH = STEPS * SWEEPS
LANES = 128
SUB = 8
PER = LANES // DEPTH
VMEM_LIMIT = 40 * 1024 * 1024


def params(**extra):
    return pltpu.CompilerParams(vmem_limit_bytes=VMEM_LIMIT, **extra)


def lane_iota(shape):
    return lax.broadcasted_iota(jnp.int32, shape, len(shape) - 1)


def roll_lanes(x, shift):
    shift = shift % LANES
    return x if shift == 0 else pltpu.roll(x, shift, x.ndim - 1)


def pack_kernel(channels, padded, cols, count_ref, value_ref, cell_ref, out_ref):
    owners, slots = cell_ref.shape
    for c in range(channels):
        out_ref[pl.ds(c, owners, stride=padded), :] = value_ref[pl.ds(c * owners, owners), :]
    owner = lax.broadcasted_iota(jnp.int32, (owners, slots), 0)
    count = jnp.zeros((owners, slots), jnp.int32)
    for d in range(owners):
        count = jnp.where(owner == d, count_ref[0, d], count)
    cell = cell_ref[...].astype(jnp.float32)
    row = jnp.floor((cell + 0.5) * (1.0 / cols))
    col = cell - row * cols
    row = jnp.where(lane_iota((owners, slots)) < count, row, -1.0)
    out_ref[pl.ds(channels, owners, stride=padded), :] = row
    out_ref[pl.ds(channels + 1, owners, stride=padded), :] = col
    for c in range(channels + 2, padded):
        out_ref[pl.ds(c, owners, stride=padded), :] = jnp.zeros((owners, slots), jnp.float32)


def unpack_kernel(channels, padded, in_ref, out_ref):
    owners = out_ref.shape[1]
    for c in range(channels):
        out_ref[c] = in_ref[pl.ds(c, owners, stride=padded), :]


def pack_strip(read, count, east, out_ref):
    for v in range(out_ref.shape[0]):
        total = None
        for s in range(min(PER, count - v * PER)):
            x = read(v * PER + s)
            x = roll_lanes(x, s * DEPTH + (DEPTH if east else 0))
            if total is None:
                total = x
            else:
                total = jnp.where(lane_iota(x.shape) >= s * DEPTH, x, total)
        out_ref[v] = total


def strip_count(rows):
    return -(-rows // PER)


def emit_strips(own_ref, west_ref, east_ref, top_ref, bottom_ref):
    rows, _, cols = own_ref.shape
    pack_strip(lambda j: own_ref[j, :, :LANES], rows, False, west_ref)
    pack_strip(lambda j: own_ref[j, :, cols - LANES :], rows, True, east_ref)
    top_ref[...] = own_ref[rows - DEPTH :]
    bottom_ref[...] = own_ref[:DEPTH]


def strip_shapes(rows, width, cols):
    strip = jax.ShapeDtypeStruct((strip_count(rows), width, LANES), jnp.float32)
    slab = jax.ShapeDtypeStruct((DEPTH, width, cols), jnp.float32)
    return (strip, strip, slab, slab)


def coef_kernel(bottom_ref, kappa_ref, own_ref, west_ref, east_ref, top_ref, low_ref):
    rows, cols = bottom_ref.shape
    part = lax.broadcasted_iota(jnp.int32, (SUB, cols), 0)
    bottom = bottom_ref[...].astype(jnp.float32)
    for j in range(rows):
        plane = jnp.where(
            part == 0,
            bottom[j : j + 1, :],
            jnp.where(part == 1, kappa_ref[0, j : j + 1, :], kappa_ref[1, j : j + 1, :]),
        )
        own_ref[j] = plane
    emit_strips(own_ref, west_ref, east_ref, top_ref, low_ref)


def ghost_kernel(where_ref, north_ref, first_ref, second_ref, south_ref, ghost_ref, west_ref, east_ref):
    depth, width, cols = north_ref.shape

    @pl.when(where_ref[0] == 1)
    def _():
        source = lax.broadcasted_iota(jnp.int32, (cols, cols), 0)
        target = lax.broadcasted_iota(jnp.int32, (cols, cols), 1)
        near = (source == where_ref[1] - target).astype(jnp.float32)
        far = (source == where_ref[1] - target + cols).astype(jnp.float32)
        first = first_ref[...].reshape(depth * width, cols)
        second = second_ref[...].reshape(depth * width, cols)
        dot = functools.partial(
            jnp.dot, preferred_element_type=jnp.float32, precision=lax.Precision.HIGHEST
        )
        mirrored = (dot(first, near) + dot(second, far)).reshape(depth, width, cols)
        for j in range(depth):
            ghost_ref[j] = mirrored[depth - 1 - j]

    @pl.when(where_ref[0] == 0)
    def _():
        ghost_ref[...] = north_ref[...]

    def read(lo):
        return lambda j: (
            south_ref[j, :, lo : lo + LANES] if j < depth else ghost_ref[j - depth, :, lo : lo + LANES]
        )

    pack_strip(read(0), 2 * depth, False, west_ref)
    pack_strip(read(cols - LANES), 2 * depth, True, east_ref)


def with_halo(own, west, east, top, low, centre_tile, where, n_lat, n_lon):
    width, cols = own.shape[1:]
    to_east = [(i, (i + 1) % n_lon) for i in range(n_lon)]
    to_west = [(b, a) for a, b in to_east]
    to_north = [(i, i + 1) for i in range(n_lat - 1)]
    to_south = [(b, a) for a, b in to_north]
    west_halo = lax.ppermute(east, "lon", to_east)
    east_halo = lax.ppermute(west, "lon", to_west)
    south = lax.ppermute(top, "lat", to_north)
    north = lax.ppermute(low, "lat", to_south)
    first_dev = (n_lat - 1) * n_lon

    def fold(tile):
        def send(block):
            return tuple(
                lax.ppermute(
                    block,
                    ("lat", "lon"),
                    [(first_dev + s, first_dev + (tile - part - s) % n_lon) for s in range(n_lon)],
                )
                for part in (0, 1)
            )

        return send

    first, second = lax.switch(centre_tile, [fold(t) for t in range(n_lon)], top)
    corner = jax.ShapeDtypeStruct((strip_count(2 * DEPTH), width, LANES), jnp.float32)
    vmem = pl.BlockSpec(memory_space=pltpu.VMEM)
    ghost, corner_west, corner_east = pl.pallas_call(
        ghost_kernel,
        out_shape=(jax.ShapeDtypeStruct((DEPTH, width, cols), jnp.float32), corner, corner),
        in_specs=[pl.BlockSpec(memory_space=pltpu.SMEM)] + [vmem] * 4,
        out_specs=(vmem,) * 3,
        compiler_params=params(),
        name="north_ghost",
    )(where, north, first, second, south)
    corner_w = lax.ppermute(corner_east, "lon", to_east)
    corner_e = lax.ppermute(corner_west, "lon", to_west)
    return (own, south, ghost, west_halo, east_halo, corner_w, corner_e)


def tile_starts(cols):
    count = max(1, -(-cols // (LANES - 2 * DEPTH)))
    if count == 1:
        return [-DEPTH]
    span = cols + 2 * DEPTH - LANES
    return [-DEPTH + (k * span) // (count - 1) for k in range(count)]


def tile_bounds(cols):
    starts = tile_starts(cols)
    inner = [
        (starts[k] + LANES - DEPTH + starts[k + 1] + DEPTH) // 2 for k in range(len(starts) - 1)
    ]
    return [0] + inner + [cols]


def tile_row(j, start, refs):
    own_ref, south_ref, north_ref, west_ref, east_ref, corner_w_ref, corner_e_ref = refs
    rows, _, cols = own_ref.shape
    if j < DEPTH:
        body, at, west, east, s = south_ref, j, corner_w_ref, corner_e_ref, j
    elif j < DEPTH + rows:
        body, at, west, east, s = own_ref, j - DEPTH, west_ref, east_ref, j - DEPTH
    else:
        at = j - DEPTH - rows
        body, west, east, s = north_ref, corner_w_ref, corner_e_ref, at + DEPTH
    out = None
    for m in range(-(-cols // LANES)):
        lo, hi = max(0, m * LANES - start), min(LANES, (m + 1) * LANES - start)
        if lo >= hi:
            continue
        piece = roll_lanes(body[at, :, m * LANES : (m + 1) * LANES], m * LANES - start)
        out = piece if out is None else jnp.where(lane_iota(piece.shape) >= lo, piece, out)
    if start < 0:
        piece = roll_lanes(west[s // PER], -start - DEPTH - (s % PER) * DEPTH)
        out = jnp.where(lane_iota(out.shape) < -start, piece, out)
    if start + LANES > cols:
        piece = roll_lanes(east[s // PER], cols - start - (s % PER) * DEPTH)
        out = jnp.where(lane_iota(out.shape) >= cols - start, piece, out)
    return out


def channel_vector(ref, group, fill):
    sub = lax.broadcasted_iota(jnp.int32, (SUB, LANES), 0)
    out = jnp.full((SUB, LANES), fill, jnp.float32)
    for s in range(SUB):
        c = group * SUB + s
        if c < ref.shape[0]:
            out = jnp.where(sub == s, ref[c], out)
    return out


def channel_level(group):
    c = lax.broadcasted_iota(jnp.int32, (SUB, LANES), 0) + group * SUB
    level = jnp.where(c < LEV, c, jnp.where(c < 2 * LEV, c - LEV, jnp.where(c == 2 * LEV, 0, LEV)))
    return level.astype(jnp.float32)


def weight_kernel(starts, groups, scale_ref, sigma_ref, *refs):
    halo_refs, (be_ref, bn_ref, q_ref, r_ref, ext_ref) = refs[:7], refs[7:]
    total = ext_ref.shape[0]
    tile = pl.program_id(0)
    for k, start in enumerate(starts):

        @pl.when(tile == k)
        def _():
            for j in range(total):
                ext_ref[j] = tile_row(j, start, halo_refs)

    levels = [channel_level(g) for g in range(groups)]
    scales = [channel_vector(scale_ref, g, 0.0) for g in range(groups)]
    sigmas = [channel_vector(sigma_ref, g, 0.0) for g in range(groups)]

    def spread(x, part):
        return jnp.broadcast_to(x[part : part + 1, :], (SUB, LANES))

    below = [jnp.zeros((SUB, LANES), jnp.float32)] * groups
    root_below = [None] * groups
    x = ext_ref[0]
    for j in range(total):
        x_north = ext_ref[j + 1] if j + 1 < total else None
        x_east = roll_lanes(x, -1)
        bottom = spread(x, 0)
        bottom_e = spread(jnp.minimum(x, x_east), 0)
        kappa_e = spread(0.5 * (x + x_east), 1)
        if x_north is not None:
            bottom_n = spread(jnp.minimum(x, x_north), 0)
            kappa_n = spread(0.5 * (x + x_north), 2)
        for g in range(groups):
            a_e = jnp.where(levels[g] < bottom_e, scales[g] * kappa_e, 0.0)
            if x_north is not None:
                a_n = jnp.where(levels[g] < bottom_n, scales[g] * kappa_n, 0.0)
            else:
                a_n = jnp.zeros((SUB, LANES), jnp.float32)
            d = 1.0 + a_e + roll_lanes(a_e, 1) + a_n + below[g]
            root = lax.rsqrt(d)
            root = root * (1.5 - 0.5 * d * root * root)
            r_ref[0, g, j] = root
            be_ref[0, g, j] = a_e * root * roll_lanes(root, -1)
            q_ref[0, g, j] = jnp.where(levels[g] < bottom, sigmas[g] * (d * root), 0.0)
            if j > 0:
                bn_ref[0, g, j - 1] = below[g] * root_below[g] * root
            below[g] = a_n
            root_below[g] = root
        x = x_north
    for g in range(groups):
        bn_ref[0, g, total - 1] = jnp.zeros((SUB, LANES), jnp.float32)


def weights(halo, length_scale, sigma, groups):
    rows, _, cols = halo[0].shape
    starts = tile_starts(cols)
    total = rows + 2 * DEPTH
    vmem = pl.BlockSpec(memory_space=pltpu.VMEM)
    smem = pl.BlockSpec(memory_space=pltpu.SMEM)
    shape = jax.ShapeDtypeStruct((len(starts), groups, total, SUB, LANES), jnp.float32)
    block = pl.BlockSpec((1, groups, total, SUB, LANES), lambda k: (k, 0, 0, 0, 0))
    cells = rows * cols * groups * SUB
    return pl.pallas_call(
        functools.partial(weight_kernel, starts, groups),
        grid=(len(starts),),
        out_shape=(shape,) * 4,
        in_specs=[smem, smem] + [vmem] * 7,
        out_specs=(block,) * 4,
        scratch_shapes=[pltpu.VMEM((total, SUB, LANES), jnp.float32)],
        compiler_params=params(),
        cost_estimate=pl.CostEstimate(flops=20 * cells, bytes_accessed=24 * cells, transcendentals=cells),
        name="weights",
    )(length_scale, sigma, *halo)


def split(x):
    high = x.astype(jnp.bfloat16)
    low = (x - high.astype(jnp.float32)).astype(jnp.bfloat16)
    return high, low


def scatter_kernel(channels, chunk, obs_ref, own_ref, west_ref, east_ref, top_ref, low_ref, left_ref, right_ref, sum_ref):
    senders, padded, slots = obs_ref.shape
    rows, _, cols = own_ref.shape
    row_iota = lax.broadcasted_iota(jnp.int32, (rows, slots), 0).astype(jnp.float32)
    col_iota = lax.broadcasted_iota(jnp.int32, (cols, slots), 0).astype(jnp.float32)

    def body(step, carry):
        for s in range(chunk):
            x = obs_ref[step * chunk + s]
            high, low = split(x)
            on_row = (row_iota == x[channels : channels + 1, :]).astype(jnp.bfloat16)
            on_col = (col_iota == x[channels + 1 : channels + 2, :]).astype(jnp.bfloat16)
            at = s * 2 * slots
            right_ref[:, at : at + slots] = on_col
            right_ref[:, at + slots : at + 2 * slots] = on_col
            for c in range(padded):
                left_ref[c * rows : (c + 1) * rows, at : at + slots] = on_row * high[c : c + 1, :]
                left_ref[c * rows : (c + 1) * rows, at + slots : at + 2 * slots] = on_row * low[c : c + 1, :]
        part = lax.dot_general(
            left_ref[...], right_ref[...], (((1,), (1,)), ((), ())), preferred_element_type=jnp.float32
        )
        for m in range(cols // LANES):
            piece = part[:, m * LANES : (m + 1) * LANES]

            @pl.when(step == 0)
            def _():
                sum_ref[m] = piece

            @pl.when(step > 0)
            def _():
                sum_ref[m] += piece

        return carry

    lax.fori_loop(0, senders // chunk, body, 0)
    for m in range(cols // LANES):
        for g in range(padded // SUB):
            for j in range(rows):
                own_ref[j, g * SUB : (g + 1) * SUB, m * LANES : (m + 1) * LANES] = sum_ref[
                    m, pl.ds(g * SUB * rows + j, SUB, stride=rows), :
                ]
    emit_strips(own_ref, west_ref, east_ref, top_ref, low_ref)


def scatter(obs, channels, rows, cols):
    senders, padded, slots = obs.shape
    chunk = 8 if senders % 8 == 0 else 1
    vmem = pl.BlockSpec(memory_space=pltpu.VMEM)
    own = jax.ShapeDtypeStruct((rows, padded, cols), jnp.float32)
    return pl.pallas_call(
        functools.partial(scatter_kernel, channels, chunk),
        out_shape=(own,) + strip_shapes(rows, padded, cols),
        in_specs=[vmem],
        out_specs=(vmem,) * 5,
        scratch_shapes=[
            pltpu.VMEM((padded * rows, chunk * 2 * slots), jnp.bfloat16),
            pltpu.VMEM((cols, chunk * 2 * slots), jnp.bfloat16),
            pltpu.VMEM((cols // LANES, padded * rows, LANES), jnp.float32),
        ],
        compiler_params=params(),
        name="scatter",
    )(obs)


def sweep_kernel(starts, bounds, sigma_ref, be_ref, bn_ref, q_ref, r_ref, *refs):
    halo_refs = refs[:7]
    fine_ref, out_ref, source_ref, even_ref, odd_ref, turn_ref = refs[7:]
    rows, _, cols = halo_refs[0].shape
    total = rows + 2 * DEPTH
    group, tile = pl.program_id(0), pl.program_id(1)
    for k, start in enumerate(starts):

        @pl.when(tile == k)
        def _():
            for j in range(total):
                even_ref[j] = tile_row(j, start, halo_refs) * q_ref[0, 0, j]

    state, other = even_ref, odd_ref
    done = 0
    for step in range(STEPS):
        for j in range(done, total - done):
            root = r_ref[0, 0, j]
            source_ref[j] = state[j] * (root * root)
        for _sweep in range(SWEEPS):
            done += 1
            here = state[done]
            south = bn_ref[0, 0, done - 1] * state[done - 1]
            for j in range(done, total - done):
                north = state[j + 1]
                to_e = be_ref[0, 0, j]
                to_n = bn_ref[0, 0, j]
                new = source_ref[j] + south + to_n * north
                new = new + (to_e * roll_lanes(here, -1) + roll_lanes(to_e * here, 1))
                other[j] = new
                south = to_n * here
                here = north
            state, other = other, state

    sub = lax.broadcasted_iota(jnp.int32, (SUB, LANES), 0) + group * SUB
    spread = jnp.zeros((SUB, LANES), jnp.float32)
    for c in range(sigma_ref.shape[0]):
        spread = jnp.where(sub == c, sigma_ref[c], spread)
    for j in range(rows):
        state[j + DEPTH] = state[j + DEPTH] * (spread * r_ref[0, 0, j + DEPTH])
    for k, start in enumerate(starts):

        @pl.when(tile == k)
        def _():
            for m in range(cols // LANES):
                lo = max(bounds[k] - m * LANES, 0)
                hi = min(bounds[k + 1] - m * LANES, LANES)
                if lo >= hi:
                    continue
                lane = lane_iota((SUB, LANES))
                for j in range(rows):
                    piece = roll_lanes(state[j + DEPTH], start - m * LANES)
                    if lo > 0:
                        piece = jnp.where(lane >= lo, piece, fine_ref[j, :, m * LANES : (m + 1) * LANES])
                    fine_ref[j, :, m * LANES : (m + 1) * LANES] = piece

    @pl.when(tile == len(starts) - 1)
    def _():
        for m in range(cols // LANES):
            for j in range(rows):
                turn_ref[pl.ds(j, SUB, stride=rows), :] = fine_ref[j, :, m * LANES : (m + 1) * LANES]
            for s in range(SUB):
                out_ref[s, :, m * LANES : (m + 1) * LANES] = turn_ref[s * rows : (s + 1) * rows, :]


def sweeps(halo, weight, sigma, channels):
    own = halo[0]
    rows, padded, cols = own.shape
    starts, bounds = tile_starts(cols), tile_bounds(cols)
    total = rows + 2 * DEPTH
    groups = padded // SUB

    def side(x):
        return pl.BlockSpec((x.shape[0], SUB, x.shape[2]), lambda g, k: (0, g, 0))

    block = pl.BlockSpec((1, 1, total, SUB, LANES), lambda g, k: (k, g, 0, 0, 0))
    scratch = pltpu.VMEM((total, SUB, LANES), jnp.float32)
    return pl.pallas_call(
        functools.partial(sweep_kernel, starts, bounds),
        grid=(groups, len(starts)),
        out_shape=(
            jax.ShapeDtypeStruct((rows, padded, cols), jnp.float32),
            jax.ShapeDtypeStruct((channels, rows, cols), jnp.float32),
        ),
        in_specs=[pl.BlockSpec(memory_space=pltpu.SMEM)] + [block] * 4 + [side(x) for x in halo],
        out_specs=(
            pl.BlockSpec((rows, SUB, cols), lambda g, k: (0, g, 0)),
            pl.BlockSpec((SUB, rows, cols), lambda g, k: (g, 0, 0)),
        ),
        scratch_shapes=[scratch, scratch, scratch, pltpu.VMEM((SUB * rows, LANES), jnp.float32)],
        compiler_params=params(),
        name="sweeps",
    )(sigma, *weight, *halo)


def gather_kernel(channels, pair, fine_ref, obs_ref, out_ref, left_ref):
    senders, padded, slots = out_ref.shape
    rows, _, cols = fine_ref.shape
    high, low = split(fine_ref[...].reshape(rows * padded, cols))
    left_ref[:, :cols] = high
    left_ref[:, cols:] = low
    at_row, at_col = channels % SUB, (channels + 1) % SUB
    col_iota = lax.broadcasted_iota(jnp.int32, (cols, slots), 0).astype(jnp.float32)

    def body(step, carry):
        hots = []
        for s in range(pair):
            col = obs_ref[step * pair + s, at_col : at_col + 1, :]
            hots.append((col_iota == col).astype(jnp.bfloat16))
        hot = jnp.concatenate(hots, axis=1)
        found = jnp.dot(
            left_ref[...], jnp.concatenate([hot, hot], axis=0), preferred_element_type=jnp.float32
        )
        for s in range(pair):
            row = jnp.broadcast_to(obs_ref[step * pair + s, at_row : at_row + 1, :], (padded, slots))
            total = jnp.zeros((padded, slots), jnp.float32)
            for j in range(rows):
                piece = found[j * padded : (j + 1) * padded, s * slots : (s + 1) * slots]
                total = jnp.where(row == float(j), piece, total)
            out_ref[step * pair + s] = total
        return carry

    lax.fori_loop(0, senders // pair, body, 0)


def gather(fine, obs, channels):
    rows, padded, cols = fine.shape
    senders, _, slots = obs.shape
    pair = 2 if senders % 2 == 0 else 1
    where_group = channels // SUB
    vmem = pl.BlockSpec(memory_space=pltpu.VMEM)
    return pl.pallas_call(
        functools.partial(gather_kernel, channels, pair),
        grid=(1,),
        out_shape=jax.ShapeDtypeStruct((senders, padded, slots), jnp.float32),
        in_specs=[
            pl.BlockSpec((rows, padded, cols), lambda i: (0, 0, 0)),
            pl.BlockSpec((senders, SUB, slots), lambda i: (0, where_group, 0)),
        ],
        out_specs=pl.BlockSpec((senders, padded, slots), lambda i: (0, 0, 0)),
        scratch_shapes=[pltpu.VMEM((rows * padded, 2 * cols), jnp.bfloat16)],
        compiler_params=params(),
        name="gather",
    )(fine, obs)


def per_device(
    obs_value, obs_cell, obs_count, bottom_level, diffusivity, partner, length_scale, sigma
):
    _, channels, owners, slots = obs_value.shape
    rows, cols = bottom_level.shape
    n_lat, n_lon = lax.axis_size("lat"), lax.axis_size("lon")
    padded = -(-(channels + 2) // SUB) * SUB
    vmem = pl.BlockSpec(memory_space=pltpu.VMEM)
    smem = pl.BlockSpec(memory_space=pltpu.SMEM)

    outgoing = pl.pallas_call(
        functools.partial(pack_kernel, channels, padded, cols),
        out_shape=jax.ShapeDtypeStruct((owners * padded, slots), jnp.float32),
        in_specs=[smem, vmem, vmem],
        out_specs=vmem,
        compiler_params=params(),
        name="pack",
    )(obs_count, obs_value.reshape(channels * owners, slots), obs_cell[0])
    arrived = lax.all_to_all(
        outgoing.reshape(owners, padded, slots), ("lat", "lon"), split_axis=0, concat_axis=0, tiled=True
    )

    n_cols = cols * n_lon
    centre = lax.rem(partner[0] + lax.axis_index("lon") * cols, n_cols)
    centre_tile, centre_col = centre // cols, centre % cols
    is_top = (lax.axis_index("lat") == n_lat - 1).astype(jnp.int32)
    where = jnp.stack([is_top, centre_col])
    around = functools.partial(
        with_halo, centre_tile=centre_tile, where=where, n_lat=n_lat, n_lon=n_lon
    )

    coef = pl.pallas_call(
        coef_kernel,
        out_shape=(jax.ShapeDtypeStruct((rows, SUB, cols), jnp.float32),) + strip_shapes(rows, SUB, cols),
        in_specs=[vmem] * 2,
        out_specs=(vmem,) * 5,
        compiler_params=params(),
        name="coefficients",
    )(bottom_level, diffusivity)
    weight = weights(around(*coef), length_scale, sigma, padded // SUB)

    field = around(*scatter(arrived, channels, rows, cols))
    fine, diffused = sweeps(field, weight, sigma, channels)
    local_fit = gather(fine, arrived, channels)
    returned = lax.all_to_all(local_fit, ("lat", "lon"), split_axis=0, concat_axis=0, tiled=True)
    obs_fit = pl.pallas_call(
        functools.partial(unpack_kernel, channels, padded),
        out_shape=jax.ShapeDtypeStruct((channels, owners, slots), jnp.float32),
        in_specs=[vmem],
        out_specs=vmem,
        compiler_params=params(),
        name="unpack",
    )(returned.reshape(owners * padded, slots))
    return obs_fit[None], diffused


def solution(mesh):
    return jax.shard_map(
        per_device,
        mesh=mesh,
        in_specs=(
            P(("lat", "lon"), None, None, None),
            P(("lat", "lon"), None, None),
            P(("lat", "lon"), None),
            P("lat", "lon"),
            P(None, "lat", "lon"),
            P("lon"),
            P(),
            P(),
        ),
        out_specs=(P(("lat", "lon"), None, None, None), P(None, "lat", "lon")),
        check_vma=False,
    )
```

```python
import functools

import jax
import jax.numpy as jnp
from jax import lax
from jax.experimental import pallas as pl
from jax.experimental.pallas import tpu as pltpu
from jax.sharding import PartitionSpec as P

LEV = 10
STEPS = 2
SWEEPS = 6
DEPTH = STEPS * SWEEPS
LANES = 128
SUB = 8
PER = LANES // DEPTH
PHASES = 3
COEFS = 3
VMEM_LIMIT = 40 * 1024 * 1024


def params(limit=VMEM_LIMIT):
    return pltpu.CompilerParams(vmem_limit_bytes=limit)


def lane_iota(shape):
    return lax.broadcasted_iota(jnp.int32, shape, len(shape) - 1)


def roll_lanes(x, shift):
    shift = shift % LANES
    return x if shift == 0 else pltpu.roll(x, shift, x.ndim - 1)


def pack_kernel(channels, padded, cols, count_ref, value_ref, cell_ref, out_ref):
    owners, slots = cell_ref.shape
    for c in range(channels):
        out_ref[pl.ds(c, owners, stride=padded), :] = value_ref[pl.ds(c * owners, owners), :]
    owner = lax.broadcasted_iota(jnp.int32, (owners, slots), 0)
    count = jnp.zeros((owners, slots), jnp.int32)
    for d in range(owners):
        count = jnp.where(owner == d, count_ref[0, d], count)
    cell = cell_ref[...].astype(jnp.float32)
    row = jnp.floor((cell + 0.5) * (1.0 / cols))
    col = cell - row * cols
    row = jnp.where(lane_iota((owners, slots)) < count, row, -1.0)
    out_ref[pl.ds(channels, owners, stride=padded), :] = row
    out_ref[pl.ds(channels + 1, owners, stride=padded), :] = col
    for c in range(channels + 2, padded):
        out_ref[pl.ds(c, owners, stride=padded), :] = jnp.zeros((owners, slots), jnp.float32)


def unpack_kernel(channels, padded, in_ref, out_ref):
    owners = out_ref.shape[1]
    for c in range(channels):
        out_ref[c] = in_ref[pl.ds(c, owners, stride=padded), :]


def split(x):
    high = x.astype(jnp.bfloat16)
    low = (x - high.astype(jnp.float32)).astype(jnp.bfloat16)
    return high, low


def phase_matrix(cols, dtype):
    shape = (cols + LANES, PHASES * LANES)
    source = lax.broadcasted_iota(jnp.int32, shape, 0)
    target = lax.broadcasted_iota(jnp.int32, shape, 1)
    w = (target % LANES) * PHASES + target // LANES
    at = jnp.where(w < DEPTH, w + cols, jnp.where(w < DEPTH + cols, w - DEPTH, w))
    return jnp.where((source == at) & (w < cols + 2 * DEPTH), 1.0, 0.0).astype(dtype)


def plain_matrix(cols, dtype):
    shape = (PHASES * LANES, cols)
    source = lax.broadcasted_iota(jnp.int32, shape, 0)
    w = lax.broadcasted_iota(jnp.int32, shape, 1) + DEPTH
    return jnp.where(source == (w % PHASES) * LANES + w // PHASES, 1.0, 0.0).astype(dtype)


def moved(x, matrix, exact=False):
    dot = functools.partial(jnp.dot, preferred_element_type=jnp.float32)
    high, low = split(x)
    out = dot(high, matrix) + dot(low, matrix)
    if exact:
        rest = (x - high.astype(jnp.float32)) - low.astype(jnp.float32)
        out = out + dot(rest.astype(jnp.bfloat16), matrix)
    return out


def mirror_matrices(cols, centre_col):
    source = lax.broadcasted_iota(jnp.int32, (cols, cols), 0)
    target = lax.broadcasted_iota(jnp.int32, (cols, cols), 1)
    near = (source == centre_col - target).astype(jnp.float32).astype(jnp.bfloat16)
    far = (source == centre_col - target + cols).astype(jnp.float32).astype(jnp.bfloat16)
    return near, far


def strip_count(rows):
    return -(-rows // PER)


class Moves:
    def __init__(self, n_lat, n_lon, centre_tile):
        self.to_east = [(i, (i + 1) % n_lon) for i in range(n_lon)]
        self.to_west = [(b, a) for a, b in self.to_east]
        self.to_north = [(i, i + 1) for i in range(n_lat - 1)]
        self.to_south = [(b, a) for a, b in self.to_north]
        self.n_lon = n_lon
        self.first = (n_lat - 1) * n_lon
        self.centre_tile = centre_tile

    def east(self, x):
        return lax.ppermute(x, "lon", self.to_east)

    def west(self, x):
        return lax.ppermute(x, "lon", self.to_west)

    def north(self, x):
        return lax.ppermute(x, "lat", self.to_north)

    def south(self, x):
        return lax.ppermute(x, "lat", self.to_south)

    def fold(self, centre_half, slab, halves):
        def pairs(tile, part):
            return [
                (self.first + s, self.first + (tile - part - s) % self.n_lon) for s in range(self.n_lon)
            ]

        def branch(tile, half):
            def run(whole, left, right):
                return (
                    lax.ppermute(whole, ("lat", "lon"), pairs(tile, 1 - half)),
                    lax.ppermute((left, right)[half], ("lat", "lon"), pairs(tile, half)),
                )

            return run

        branches = [branch(t, h) for t in range(self.n_lon) for h in (0, 1)]
        return lax.switch(self.centre_tile * 2 + centre_half, branches, slab, *halves)


def scatter_kernel(channels, chunk, obs_ref, bottom_ref, kappa_ref, *refs):
    own_ref, top_ref, low_ref = refs[:3]
    half_refs, (left_ref, right_ref, sum_ref) = refs[3:-3], refs[-3:]
    senders, padded, slots = obs_ref.shape
    rows, _, cols = own_ref.shape
    row_iota = lax.broadcasted_iota(jnp.int32, (rows, slots), 0).astype(jnp.float32)
    col_iota = lax.broadcasted_iota(jnp.int32, (cols, slots), 0).astype(jnp.float32)

    def body(step, carry):
        for s in range(chunk):
            x = obs_ref[step * chunk + s]
            high, low = split(x)
            on_row = (row_iota == x[channels : channels + 1, :]).astype(jnp.bfloat16)
            on_col = (col_iota == x[channels + 1 : channels + 2, :]).astype(jnp.bfloat16)
            at = s * 2 * slots
            right_ref[:, at : at + slots] = on_col
            right_ref[:, at + slots : at + 2 * slots] = on_col
            for c in range(channels):
                left_ref[c * rows : (c + 1) * rows, at : at + slots] = on_row * high[c : c + 1, :]
                left_ref[c * rows : (c + 1) * rows, at + slots : at + 2 * slots] = on_row * low[c : c + 1, :]
        part = lax.dot_general(
            left_ref[...], right_ref[...], (((1,), (1,)), ((), ())), preferred_element_type=jnp.float32
        )
        for m in range(cols // LANES):
            piece = part[:, m * LANES : (m + 1) * LANES]

            @pl.when(step == 0)
            def _():
                sum_ref[m, : channels * rows] = piece

            @pl.when(step > 0)
            def _():
                sum_ref[m, : channels * rows] += piece

        return carry

    lax.fori_loop(0, senders // chunk, body, 0)
    coefs = [bottom_ref[...].astype(jnp.float32), kappa_ref[0], kappa_ref[1]]
    for m in range(cols // LANES):
        at = slice(m * LANES, (m + 1) * LANES)
        for i, coef in enumerate(coefs):
            sum_ref[m, (channels + i) * rows : (channels + i + 1) * rows] = coef[:, at]
        for g in range(padded // SUB):
            for j in range(rows):
                own_ref[j, g * SUB : (g + 1) * SUB, at] = sum_ref[
                    m, pl.ds(g * SUB * rows + j, SUB, stride=rows), :
                ]
        top_ref[m] = own_ref[rows - DEPTH :, :, at]
        half_refs[m][...] = own_ref[rows - DEPTH :, :, at]
        low_ref[m] = own_ref[:DEPTH, :, at]


def scatter(obs, bottom_level, diffusivity, channels):
    senders, padded, slots = obs.shape
    rows, cols = bottom_level.shape
    tiles = cols // LANES
    chunk = 8 if senders % 8 == 0 else 1
    vmem = pl.BlockSpec(memory_space=pltpu.VMEM)
    half = jax.ShapeDtypeStruct((DEPTH, padded, LANES), jnp.float32)
    slab = jax.ShapeDtypeStruct((tiles, DEPTH, padded, LANES), jnp.float32)
    shapes = [jax.ShapeDtypeStruct((rows, padded, cols), jnp.float32), slab, slab] + [half] * tiles
    return pl.pallas_call(
        functools.partial(scatter_kernel, channels, chunk),
        out_shape=tuple(shapes),
        in_specs=[vmem] * 3,
        out_specs=(vmem,) * len(shapes),
        scratch_shapes=[
            pltpu.VMEM((channels * rows, chunk * 2 * slots), jnp.bfloat16),
            pltpu.VMEM((cols, chunk * 2 * slots), jnp.bfloat16),
            pltpu.VMEM((tiles, padded * rows, LANES), jnp.float32),
        ],
        compiler_params=params(),
        cost_estimate=pl.CostEstimate(
            flops=4 * senders * slots * padded * rows * cols, bytes_accessed=0, transcendentals=0
        ),
        name="scatter",
    )(obs, bottom_level, diffusivity)


def pack_strip(read, count, east, out_ref):
    for v in range(out_ref.shape[0]):
        total = None
        for s in range(min(PER, count - v * PER)):
            x = roll_lanes(read(v * PER + s), s * DEPTH + (DEPTH if east else 0))
            total = x if total is None else jnp.where(lane_iota(x.shape) >= s * DEPTH, x, total)
        out_ref[v] = total


def ghost_kernel(where_ref, south_ref, own_ref, north_ref, whole_ref, part_ref, ghost_ref, west_ref, east_ref):
    tiles, depth, width, _ = ghost_ref.shape
    cols = tiles * LANES

    for half in (0, 1):

        @pl.when((where_ref[0] == 1) & (where_ref[1] // LANES == half))
        def _():
            near, far = mirror_matrices(cols, where_ref[1])
            whole = [whole_ref[m].reshape(depth * width, LANES) for m in range(tiles)]
            part = part_ref[...].reshape(depth * width, LANES)
            if half == 0:
                x, matrix = [part] + whole, jnp.concatenate([near[:LANES], far], axis=0)
            else:
                x, matrix = whole + [part], jnp.concatenate([near, far[LANES:]], axis=0)
            mirrored = moved(jnp.concatenate(x, axis=1), matrix, exact=True)
            for m in range(tiles):
                block = mirrored[:, m * LANES : (m + 1) * LANES].reshape(depth, width, LANES)
                for j in range(depth):
                    ghost_ref[m, j] = block[depth - 1 - j]

    @pl.when(where_ref[0] == 0)
    def _():
        ghost_ref[...] = north_ref[...]

    rows = own_ref.shape[0]

    def read(m):
        def at(j):
            if j < depth:
                return south_ref[m, j]
            if j >= depth + rows:
                return ghost_ref[m, j - depth - rows]
            return own_ref[j - depth, :, m * LANES : (m + 1) * LANES]

        return at

    pack_strip(read(0), rows + 2 * depth, False, west_ref)
    pack_strip(read(tiles - 1), rows + 2 * depth, True, east_ref)


def field_ghosts(where, south, own, north, whole, part):
    width = own.shape[1]
    count = own.shape[0] + 2 * DEPTH
    strip = jax.ShapeDtypeStruct((strip_count(count), width, LANES), jnp.float32)
    vmem = pl.BlockSpec(memory_space=pltpu.VMEM)
    return pl.pallas_call(
        ghost_kernel,
        out_shape=(jax.ShapeDtypeStruct(south.shape, jnp.float32), strip, strip),
        in_specs=[pl.BlockSpec(memory_space=pltpu.SMEM)] + [vmem] * 5,
        out_specs=(vmem,) * 3,
        compiler_params=params(),
        name="field_ghosts",
    )(where, south, own, north, whole, part)


def east_of(xs, m):
    return xs[m + 1] if m + 1 < PHASES else roll_lanes(xs[0], -1)


def west_of(xs, m):
    return xs[m - 1] if m > 0 else roll_lanes(xs[PHASES - 1], 1)


def cell_terms(first, wide_ref, cell_ref):
    total = wide_ref.shape[1] // SUB

    def coef(i, m, skip=0):
        return wide_ref[m, pl.ds(first + i + skip * SUB, total - skip, stride=SUB), :]

    lon = [coef(1, m) for m in range(PHASES)]
    bottom = [coef(0, m) for m in range(PHASES)]
    for m in range(PHASES):
        cell_ref[0, m] = bottom[m]
        cell_ref[1, m] = jnp.minimum(bottom[m], east_of(bottom, m))
        cell_ref[2, m] = 0.5 * (lon[m] + east_of(lon, m))
        cell_ref[3, m, : total - 1] = jnp.minimum(bottom[m][: total - 1], coef(0, m, 1))
        cell_ref[4, m, : total - 1] = 0.5 * (coef(2, m)[: total - 1] + coef(2, m, 1))
        cell_ref[3, m, total - 1 :] = jnp.zeros((1, LANES), jnp.float32)
        cell_ref[4, m, total - 1 :] = jnp.zeros((1, LANES), jnp.float32)


def make_weights(level, scale, sigma, cell_ref, wide_ref, be_ref, bn_ref, root_ref, state_ref):
    total = be_ref.shape[0]
    zero = jnp.zeros((SUB, LANES), jnp.float32)
    below, root_below = [zero] * PHASES, [zero] * PHASES
    for j in range(total):

        def spread(i, m):
            return jnp.broadcast_to(cell_ref[i, m, j : j + 1, :], (SUB, LANES))

        a_e = [jnp.where(level < spread(1, m), scale * spread(2, m), 0.0) for m in range(PHASES)]
        a_n = [jnp.where(level < spread(3, m), scale * spread(4, m), 0.0) for m in range(PHASES)]
        root = []
        for m in range(PHASES):
            d = 1.0 + a_e[m] + west_of(a_e, m) + a_n[m] + below[m]
            x = lax.rsqrt(d)
            x = x * (1.5 - 0.5 * d * x * x)
            root.append(x)
            root_ref[j, m] = x
            start = jnp.where(level < spread(0, m), sigma * (d * x), 0.0)
            state_ref[j, m] = wide_ref[m, j * SUB : (j + 1) * SUB, :] * start
        for m in range(PHASES):
            be_ref[j, m] = a_e[m] * root[m] * east_of(root, m)
            if j > 0:
                bn_ref[j - 1, m] = below[m] * root_below[m] * root[m]
        below, root_below = a_n, root
    for m in range(PHASES):
        bn_ref[total - 1, m] = zero


def sweep_kernel(coef_at, scale_ref, sigma_ref, south_ref, own_ref, north_ref, west_ref, east_ref, *refs):
    fine_ref, out_ref, window_ref, wide_ref, to_phase_ref, to_plain_ref, cell_ref = refs[:7]
    be_ref, bn_ref, root_ref, source_ref, even_ref, odd_ref, turn_ref = refs[7:]
    rows, _, cols = own_ref.shape
    tiles = cols // LANES
    total = rows + 2 * DEPTH
    every = range(PHASES)
    step = pl.program_id(0)
    group = pl.num_programs(0) - 1 - step

    @pl.when(step == 0)
    def _():
        to_phase_ref[...] = phase_matrix(cols, jnp.float32).astype(jnp.bfloat16)
        to_plain_ref[...] = plain_matrix(cols, jnp.float32).astype(jnp.bfloat16)

    lane = lane_iota((SUB, LANES))
    for j in range(total):
        at = slice(j * SUB, (j + 1) * SUB)
        if DEPTH <= j < DEPTH + rows:
            window_ref[at, :cols] = own_ref[j - DEPTH]
        else:
            ref, i = (south_ref, j) if j < DEPTH else (north_ref, j - DEPTH - rows)
            for m in range(tiles):
                window_ref[at, m * LANES : (m + 1) * LANES] = ref[m, i]
        west = roll_lanes(west_ref[j // PER], -(j % PER) * DEPTH)
        east = roll_lanes(east_ref[j // PER], DEPTH - (j % PER) * DEPTH)
        side = jnp.where(lane < DEPTH, west, east)
        window_ref[at, cols:] = jnp.where(lane < 2 * DEPTH, side, 0.0)

    @pl.when(step == 0)
    def _():
        wide = moved(window_ref[...], to_phase_ref[...], exact=True)
        for m in every:
            wide_ref[m] = wide[:, m * LANES : (m + 1) * LANES]
        cell_terms(coef_at, wide_ref, cell_ref)

    @pl.when(step > 0)
    def _():
        wide = moved(window_ref[...], to_phase_ref[...])
        for m in every:
            wide_ref[m] = wide[:, m * LANES : (m + 1) * LANES]

    c = lax.broadcasted_iota(jnp.int32, (SUB, LANES), 0) + group * SUB
    level = jnp.where(c < LEV, c, jnp.where(c < 2 * LEV, c - LEV, jnp.where(c == 2 * LEV, 0, LEV)))
    scale, sigma = (jnp.zeros((SUB, LANES), jnp.float32) for _ in range(2))
    for i in range(sigma_ref.shape[0]):
        scale = jnp.where(c == i, scale_ref[i], scale)
        sigma = jnp.where(c == i, sigma_ref[i], sigma)
    make_weights(
        level.astype(jnp.float32), scale, sigma, cell_ref, wide_ref, be_ref, bn_ref, root_ref, even_ref
    )

    state, other = even_ref, odd_ref
    done = 0
    for _step in range(STEPS):
        for j in range(done, total - done):
            for m in every:
                root = root_ref[j, m]
                source_ref[j, m] = state[j, m] * (root * root)
        for _sweep in range(SWEEPS):
            done += 1
            here = [state[done, m] for m in every]
            south = [bn_ref[done - 1, m] * state[done - 1, m] for m in every]
            for j in range(done, total - done):
                north = [state[j + 1, m] for m in every]
                to_e = [be_ref[j, m] for m in every]
                to_n = [bn_ref[j, m] for m in every]
                flow = [to_e[m] * here[m] for m in every]
                for m in every:
                    new = source_ref[j, m] + south[m] + to_n[m] * north[m]
                    other[j, m] = new + (to_e[m] * east_of(here, m) + west_of(flow, m))
                south = [to_n[m] * here[m] for m in every]
                here = north
            state, other = other, state

    for j in range(rows):
        for m in every:
            window_ref[j * SUB : (j + 1) * SUB, m * LANES : (m + 1) * LANES] = state[j + DEPTH, m] * (
                sigma * root_ref[j + DEPTH, m]
            )
    plain = moved(window_ref[: rows * SUB], to_plain_ref[...])
    fine_ref[...] = plain.reshape(rows, SUB, cols)
    for m in range(tiles):
        for j in range(rows):
            turn_ref[pl.ds(j, SUB, stride=rows), :] = fine_ref[j, :, m * LANES : (m + 1) * LANES]
        for s in range(SUB):
            out_ref[s, :, m * LANES : (m + 1) * LANES] = turn_ref[s * rows : (s + 1) * rows, :]


def sweeps(south, own, north, west, east, length_scale, sigma, channels):
    rows, padded, cols = own.shape
    total = rows + 2 * DEPTH
    groups = padded // SUB
    last = groups - 1
    smem = pl.BlockSpec(memory_space=pltpu.SMEM)

    def body(x):
        return pl.BlockSpec((x.shape[0], SUB, x.shape[2]), lambda g: (0, last - g, 0))

    def slab(x):
        return pl.BlockSpec((x.shape[0], x.shape[1], SUB, LANES), lambda g: (0, 0, last - g, 0))

    plane = pltpu.VMEM((total, PHASES, SUB, LANES), jnp.float32)
    return pl.pallas_call(
        functools.partial(sweep_kernel, channels % SUB),
        grid=(groups,),
        out_shape=(
            jax.ShapeDtypeStruct((rows, padded, cols), jnp.float32),
            jax.ShapeDtypeStruct((channels, rows, cols), jnp.float32),
        ),
        in_specs=[smem, smem, slab(south), body(own), slab(north), body(west), body(east)],
        out_specs=(
            pl.BlockSpec((rows, SUB, cols), lambda g: (0, last - g, 0)),
            pl.BlockSpec((SUB, rows, cols), lambda g: (last - g, 0, 0)),
        ),
        scratch_shapes=[
            pltpu.VMEM((total * SUB, cols + LANES), jnp.float32),
            pltpu.VMEM((PHASES, total * SUB, LANES), jnp.float32),
            pltpu.VMEM((cols + LANES, PHASES * LANES), jnp.bfloat16),
            pltpu.VMEM((PHASES * LANES, cols), jnp.bfloat16),
            pltpu.VMEM((5, PHASES, total, LANES), jnp.float32),
        ]
        + [plane] * 6
        + [pltpu.VMEM((SUB * rows, LANES), jnp.float32)],
        compiler_params=params(),
        name="sweeps",
    )(length_scale, sigma, south, own, north, west, east)


def gather_kernel(channels, pair, fine_ref, obs_ref, out_ref, left_ref):
    senders, padded, slots = out_ref.shape
    rows, _, cols = fine_ref.shape
    high, low = split(fine_ref[...].reshape(rows * padded, cols))
    left_ref[:, :cols] = high
    left_ref[:, cols:] = low
    at_row, at_col = channels % SUB, (channels + 1) % SUB
    col_iota = lax.broadcasted_iota(jnp.int32, (cols, slots), 0).astype(jnp.float32)

    def body(step, carry):
        hots = []
        for s in range(pair):
            col = obs_ref[step * pair + s, at_col : at_col + 1, :]
            hots.append((col_iota == col).astype(jnp.bfloat16))
        hot = jnp.concatenate(hots, axis=1)
        found = jnp.dot(
            left_ref[...], jnp.concatenate([hot, hot], axis=0), preferred_element_type=jnp.float32
        )
        for s in range(pair):
            row = jnp.broadcast_to(obs_ref[step * pair + s, at_row : at_row + 1, :], (padded, slots))
            total = jnp.zeros((padded, slots), jnp.float32)
            for j in range(rows):
                piece = found[j * padded : (j + 1) * padded, s * slots : (s + 1) * slots]
                total = jnp.where(row == float(j), piece, total)
            out_ref[step * pair + s] = total
        return carry

    lax.fori_loop(0, senders // pair, body, 0)


def gather(fine, obs, channels):
    rows, padded, cols = fine.shape
    senders, _, slots = obs.shape
    pair = 2 if senders % 2 == 0 else 1
    where_group = channels // SUB
    vmem = pl.BlockSpec(memory_space=pltpu.VMEM)
    return pl.pallas_call(
        functools.partial(gather_kernel, channels, pair),
        grid=(1,),
        out_shape=jax.ShapeDtypeStruct((senders, padded, slots), jnp.float32),
        in_specs=[
            pl.BlockSpec((rows, padded, cols), lambda i: (0, 0, 0)),
            pl.BlockSpec((senders, SUB, slots), lambda i: (0, where_group, 0)),
        ],
        out_specs=pl.BlockSpec((senders, padded, slots), lambda i: (0, 0, 0)),
        scratch_shapes=[pltpu.VMEM((rows * padded, 2 * cols), jnp.bfloat16)],
        compiler_params=params(),
        name="gather",
    )(fine, obs)


def per_device(
    obs_value, obs_cell, obs_count, bottom_level, diffusivity, partner, length_scale, sigma
):
    _, channels, owners, slots = obs_value.shape
    rows, cols = bottom_level.shape
    n_lat, n_lon = lax.axis_size("lat"), lax.axis_size("lon")
    padded = -(-(channels + COEFS) // SUB) * SUB
    vmem = pl.BlockSpec(memory_space=pltpu.VMEM)
    smem = pl.BlockSpec(memory_space=pltpu.SMEM)

    outgoing = pl.pallas_call(
        functools.partial(pack_kernel, channels, padded, cols),
        grid=(1,),
        out_shape=jax.ShapeDtypeStruct((owners * padded, slots), jnp.float32),
        in_specs=[
            smem,
            pl.BlockSpec((channels * owners, slots), lambda i: (0, 0)),
            pl.BlockSpec((owners, slots), lambda i: (0, 0)),
        ],
        out_specs=vmem,
        compiler_params=params(60 * 1024 * 1024),
        name="pack",
    )(obs_count, obs_value.reshape(channels * owners, slots), obs_cell[0])
    arrived = lax.all_to_all(
        outgoing.reshape(owners, padded, slots), ("lat", "lon"), split_axis=0, concat_axis=0, tiled=True
    )

    centre = lax.rem(partner[0] + lax.axis_index("lon") * cols, cols * n_lon)
    centre_col = centre % cols
    is_top = (lax.axis_index("lat") == n_lat - 1).astype(jnp.int32)
    where = jnp.stack([is_top, centre_col])
    moves = Moves(n_lat, n_lon, centre // cols)

    own, top, low, *halves = scatter(arrived, bottom_level, diffusivity, channels)
    south, north = moves.north(top), moves.south(low)
    whole, part = moves.fold(centre_col // LANES, top, halves)
    ghost, west, east = field_ghosts(where, south, own, north, whole, part)
    fine, diffused = sweeps(
        south, own, ghost, moves.east(east), moves.west(west), length_scale, sigma, channels
    )
    local_fit = gather(fine, arrived, channels)
    returned = lax.all_to_all(local_fit, ("lat", "lon"), split_axis=0, concat_axis=0, tiled=True)
    obs_fit = pl.pallas_call(
        functools.partial(unpack_kernel, channels, padded),
        out_shape=jax.ShapeDtypeStruct((channels, owners, slots), jnp.float32),
        in_specs=[vmem],
        out_specs=vmem,
        compiler_params=params(),
        name="unpack",
    )(returned.reshape(owners * padded, slots))
    return obs_fit[None], diffused


def solution(mesh):
    return jax.shard_map(
        per_device,
        mesh=mesh,
        in_specs=(
            P(("lat", "lon"), None, None, None),
            P(("lat", "lon"), None, None),
            P(("lat", "lon"), None),
            P("lat", "lon"),
            P(None, "lat", "lon"),
            P("lon"),
            P(),
            P(),
        ),
        out_specs=(P(("lat", "lon"), None, None, None), P(None, "lat", "lon")),
        check_vma=False,
    )
```

```python
import functools

import jax
import jax.numpy as jnp
from jax import lax
from jax.experimental import pallas as pl
from jax.experimental.pallas import tpu as pltpu
from jax.sharding import PartitionSpec as P

LEV = 10
STEPS = 2
SWEEPS = 6
DEPTH = STEPS * SWEEPS
LANES = 128
SUB = 8
PER = LANES // DEPTH
MARGIN = -(-DEPTH // SUB) * SUB
COEFS = 3
MEGA = 1024 * 1024


def params(limit=8):
    return pltpu.CompilerParams(vmem_limit_bytes=limit * MEGA)


def lane_iota(shape):
    return lax.broadcasted_iota(jnp.int32, shape, len(shape) - 1)


def roll_lanes(x, shift):
    shift = shift % LANES
    return x if shift == 0 else pltpu.roll(x, shift, x.ndim - 1)


def pack_kernel(channels, padded, cols, count_ref, value_ref, cell_ref, out_ref):
    owners, slots = cell_ref.shape
    for c in range(channels):
        out_ref[pl.ds(c, owners, stride=padded), :] = value_ref[pl.ds(c * owners, owners), :]
    owner = lax.broadcasted_iota(jnp.int32, (owners, slots), 0)
    count = jnp.zeros((owners, slots), jnp.int32)
    for d in range(owners):
        count = jnp.where(owner == d, count_ref[0, d], count)
    cell = cell_ref[...].astype(jnp.float32)
    row = jnp.floor((cell + 0.5) * (1.0 / cols))
    col = cell - row * cols
    row = jnp.where(lane_iota((owners, slots)) < count, row, -1.0)
    out_ref[pl.ds(channels, owners, stride=padded), :] = row
    out_ref[pl.ds(channels + 1, owners, stride=padded), :] = col
    for c in range(channels + 2, padded):
        out_ref[pl.ds(c, owners, stride=padded), :] = jnp.zeros((owners, slots), jnp.float32)


def unpack_kernel(channels, padded, in_ref, out_ref):
    owners = out_ref.shape[1]
    for c in range(channels):
        out_ref[c] = in_ref[pl.ds(c, owners, stride=padded), :]


def layout(cols, groups):
    window = cols + 2 * DEPTH
    phases = -(-window // (LANES // groups))
    return phases, -(-window // phases), -(-phases // groups)


def split(x):
    high = x.astype(jnp.bfloat16)
    low = (x - high.astype(jnp.float32)).astype(jnp.bfloat16)
    return high, low


def turned_window(cols, groups, group, n):
    phases, part, _ = layout(cols, groups)
    block = n // LANES
    lane = lax.rem(n - block * LANES + (LANES - group * part % LANES), LANES)
    i = lane // part
    phase = block * groups + i
    return jnp.where((i < groups) & (phase < phases), (lane - i * part) * phases + phase, -1)


def window_source(cols, w):
    at = jnp.where(w < DEPTH, w + cols, jnp.where(w < DEPTH + cols, w - DEPTH, w))
    return jnp.where((w >= 0) & (w < cols + 2 * DEPTH), at, -1)


def moved(x, matrix, exact=False):
    dot = functools.partial(jnp.dot, preferred_element_type=jnp.float32)
    high, low = split(x)
    parts = [high, low]
    if exact:
        rest = (x - high.astype(jnp.float32)) - low.astype(jnp.float32)
        parts.append(rest.astype(jnp.bfloat16))
    return dot(jnp.concatenate(parts, axis=1), jnp.concatenate([matrix] * len(parts), axis=0))


def part_starts(cols):
    return DEPTH, cols - DEPTH - LANES


def mirror_source(cols, centre_col, kind, w):
    column = centre_col + DEPTH - w
    left, right = part_starts(cols)
    in_part = jnp.where(kind == 0, column - left, column + cols - right)
    in_whole = jnp.where(kind == 0, column + cols, column)
    at_whole = jnp.where(in_whole < 0, cols + DEPTH + in_whole, in_whole + jnp.where(in_whole < cols, 0, DEPTH))
    from_whole = (in_whole >= -DEPTH) & (in_whole < cols + DEPTH)
    at = jnp.where(from_whole, at_whole, cols + LANES + in_part)
    return jnp.where((w >= 0) & (w < cols + 2 * DEPTH), at, -1)


def fill_tables(cols, where_ref, phase_ref, plain_ref, mirror_ref):
    is_top, centre_col, kind = where_ref[0], where_ref[1], where_ref[2]
    groups = phase_ref.shape[0]
    phases, part, _ = layout(cols, groups)

    def lanes_of(ref):
        return lax.broadcasted_iota(jnp.int32, (1, ref.shape[-1]), 1)

    def hot(ref, at):
        source = lax.broadcasted_iota(jnp.int32, ref.shape[-2:], 0)
        return jnp.where(source == at, 1.0, 0.0).astype(jnp.bfloat16)

    for g in range(groups):
        w = turned_window(cols, groups, g, lanes_of(phase_ref))
        phase_ref[g] = hot(phase_ref, window_source(cols, w))
        w = lanes_of(plain_ref) + DEPTH
        phase, lane = w % phases, w // phases
        at = ((phase % groups + g) * part + lane) % LANES
        plain_ref[g] = hot(plain_ref, phase // groups * LANES + at)

    @pl.when(is_top == 1)
    def _():
        for g in range(groups):
            w = turned_window(cols, groups, g, lanes_of(mirror_ref))
            mirror_ref[g] = hot(mirror_ref, mirror_source(cols, centre_col, kind, w))


def strip_count(rows, width=DEPTH):
    return -(-rows // (LANES // width))


def pack_strip(read, count, first, out_ref):
    for v in range(out_ref.shape[0]):
        total = None
        for s in range(min(PER, count - v * PER)):
            x = roll_lanes(read(v * PER + s), s * DEPTH - first)
            total = x if total is None else jnp.where(lane_iota(x.shape) >= s * DEPTH, x, total)
        out_ref[v] = total


def halo_lanes(west, at_west, east, at_east, at=0):
    split_at = lane_iota(west.shape) < at + DEPTH
    return jnp.where(split_at, roll_lanes(west, at - at_west), roll_lanes(east, at + DEPTH - at_east))


def slab_kernel(own_ref, west_ref, east_ref, top_ref, low_ref):
    rows, _, cols = own_ref.shape
    tiles, per = cols // LANES, PER // 2
    for ref, first in ((top_ref, rows - DEPTH), (low_ref, 0)):
        for m in range(tiles):
            ref[m * DEPTH : (m + 1) * DEPTH] = own_ref[first : first + DEPTH, :, m * LANES : (m + 1) * LANES]
        for v in range(ref.shape[0] - tiles * DEPTH):
            total = None
            for s in range(min(per, DEPTH - v * per)):
                i, at = divmod(first + v * per + s, PER)
                x = halo_lanes(west_ref[i], at * DEPTH, east_ref[i], at * DEPTH, s * 2 * DEPTH)
                total = x if s == 0 else jnp.where(lane_iota(x.shape) >= s * 2 * DEPTH, x, total)
            ref[tiles * DEPTH + v] = total


def slabs(own, west, east):
    _, width, cols = own.shape
    count = cols // LANES * DEPTH + strip_count(DEPTH, 2 * DEPTH)
    vmem = pl.BlockSpec(memory_space=pltpu.VMEM)
    return pl.pallas_call(
        slab_kernel,
        out_shape=(jax.ShapeDtypeStruct((count, width, LANES), jnp.float32),) * 2,
        in_specs=[vmem] * 3,
        out_specs=(vmem,) * 2,
        compiler_params=params(),
        name="slabs",
    )(own, west, east)


class Moves:
    def __init__(self, n_lat, n_lon, centre_tile):
        self.to_east = [(i, (i + 1) % n_lon) for i in range(n_lon)]
        self.to_west = [(b, a) for a, b in self.to_east]
        self.to_north = [(i, i + 1) for i in range(n_lat - 1)]
        self.to_south = [(b, a) for a, b in self.to_north]
        self.n_lon = n_lon
        self.first = (n_lat - 1) * n_lon
        self.centre_tile = centre_tile

    def east(self, x):
        return lax.ppermute(x, "lon", self.to_east)

    def west(self, x):
        return lax.ppermute(x, "lon", self.to_west)

    def north(self, x):
        return lax.ppermute(x, "lat", self.to_north)

    def south(self, x):
        return lax.ppermute(x, "lat", self.to_south)

    def slabs(self, kind, top, low, parts):
        def pairs(tile, part):
            return [
                (self.first + s, self.first + (tile - part - s) % self.n_lon) for s in range(self.n_lon)
            ]

        def branch(tile, kind):
            def run(top, low, parts):
                part = lax.ppermute(parts[kind], ("lat", "lon"), pairs(tile, kind))
                part, slab = lax.optimization_barrier((part, top))
                whole = lax.ppermute(slab, ("lat", "lon"), pairs(tile, 1 - kind))
                return self.north(top), self.south(low), whole, part

            return run

        branches = [branch(t, k) for t in range(self.n_lon) for k in (0, 1)]
        return lax.switch(self.centre_tile * 2 + kind, branches, top, low, parts)


def scatter_kernel(channels, chunk, obs_ref, bottom_ref, kappa_ref, *refs):
    own_ref, west_ref, east_ref = refs[:3]
    part_refs, (left_ref, right_ref, sum_ref) = refs[3:5], refs[5:]
    senders, padded, slots = obs_ref.shape
    rows, _, cols = own_ref.shape
    row_iota = lax.broadcasted_iota(jnp.int32, (rows, slots), 0).astype(jnp.float32)
    col_iota = lax.broadcasted_iota(jnp.int32, (cols, slots), 0).astype(jnp.float32)

    def body(step, carry):
        for s in range(chunk):
            x = obs_ref[step * chunk + s]
            high, low = split(x)
            on_row = (row_iota == x[channels : channels + 1, :]).astype(jnp.bfloat16)
            on_col = (col_iota == x[channels + 1 : channels + 2, :]).astype(jnp.bfloat16)
            at = s * 2 * slots
            right_ref[:, at : at + slots] = on_col
            right_ref[:, at + slots : at + 2 * slots] = on_col
            for c in range(channels):
                left_ref[c * rows : (c + 1) * rows, at : at + slots] = on_row * high[c : c + 1, :]
                left_ref[c * rows : (c + 1) * rows, at + slots : at + 2 * slots] = on_row * low[c : c + 1, :]
        part = lax.dot_general(
            left_ref[...], right_ref[...], (((1,), (1,)), ((), ())), preferred_element_type=jnp.float32
        )
        for m in range(cols // LANES):
            piece = part[:, m * LANES : (m + 1) * LANES]

            @pl.when(step == 0)
            def _():
                sum_ref[m, : channels * rows] = piece

            @pl.when(step > 0)
            def _():
                sum_ref[m, : channels * rows] += piece

        return carry

    lax.fori_loop(0, senders // chunk, body, 0)
    coefs = [bottom_ref[...].astype(jnp.float32), kappa_ref[0], kappa_ref[1]]
    for m in range(cols // LANES):
        at = slice(m * LANES, (m + 1) * LANES)
        for i, coef in enumerate(coefs):
            sum_ref[m, (channels + i) * rows : (channels + i + 1) * rows] = coef[:, at]
        for g in range(padded // SUB):
            for j in range(rows):
                own_ref[j, g * SUB : (g + 1) * SUB, at] = sum_ref[
                    m, pl.ds(g * SUB * rows + j, SUB, stride=rows), :
                ]
    pack_strip(lambda j: own_ref[j, :, :LANES], rows, 0, west_ref)
    pack_strip(lambda j: own_ref[j, :, cols - LANES :], rows, LANES - DEPTH, east_ref)
    for ref, start in zip(part_refs, part_starts(cols)):
        m, shift = divmod(start, LANES)
        for j in range(DEPTH):
            x = own_ref[rows - DEPTH + j, :, m * LANES : (m + 1) * LANES]
            y = own_ref[rows - DEPTH + j, :, (m + 1) * LANES : (m + 2) * LANES]
            here = lane_iota(x.shape) < LANES - shift
            ref[j] = jnp.where(here, roll_lanes(x, -shift), roll_lanes(y, -shift))


def scatter(obs, bottom_level, diffusivity, channels):
    senders, padded, slots = obs.shape
    rows, cols = bottom_level.shape
    tiles = cols // LANES
    chunk = 8 if senders % 8 == 0 else 1
    vmem = pl.BlockSpec(memory_space=pltpu.VMEM)
    side = (strip_count(rows), padded, LANES)
    part = (DEPTH, padded, LANES)
    shapes = [(rows, padded, cols), side, side, part, part]
    shapes = [jax.ShapeDtypeStruct(shape, jnp.float32) for shape in shapes]
    return pl.pallas_call(
        functools.partial(scatter_kernel, channels, chunk),
        out_shape=tuple(shapes),
        in_specs=[vmem] * 3,
        out_specs=(vmem,) * len(shapes),
        scratch_shapes=[
            pltpu.VMEM((channels * rows, chunk * 2 * slots), jnp.bfloat16),
            pltpu.VMEM((cols, chunk * 2 * slots), jnp.bfloat16),
            pltpu.VMEM((tiles, padded * rows, LANES), jnp.float32),
        ],
        compiler_params=params(14),
        cost_estimate=pl.CostEstimate(
            flops=4 * senders * slots * padded * rows * cols, bytes_accessed=0, transcendentals=0
        ),
        name="scatter",
    )(obs, bottom_level, diffusivity)


def east_of(xs, m):
    return xs[m + 1] if m + 1 < len(xs) else roll_lanes(xs[0], -1)


def west_of(xs, m):
    return xs[m - 1] if m > 0 else roll_lanes(xs[-1], 1)


def slab_row(ref, j, cols):
    tiles, per = cols // LANES, PER // 2
    side = roll_lanes(ref[tiles * DEPTH + j // per], -(j % per) * 2 * DEPTH)
    side = jnp.where(lane_iota(side.shape) < 2 * DEPTH, side, 0.0)
    return [ref[m * DEPTH + j] for m in range(tiles)] + [side]


def part_of_lane(first, part, shape):
    return lax.rem(lane_iota(shape) + (LANES - first % LANES), LANES) // part


def cell_terms(coef_at, part, wide_ref, coef_ref, cell_ref):
    groups = wide_ref.shape[0]
    _, count, total, _ = cell_ref.shape
    which = part_of_lane(0, part, (total, LANES))
    for i in range(COEFS):
        for m in range(count):
            block, turn = divmod(m, groups)
            x = wide_ref[groups - 1, block, pl.ds(coef_at + i, total, stride=SUB), :]
            first = (groups - 1 + turn) * part
            out = jnp.zeros_like(x)
            for g in range(groups):
                out = jnp.where(which == g, roll_lanes(x, g * part - first), out)
            coef_ref[i, m, :total] = out
            coef_ref[i, m, total:] = jnp.zeros((SUB, LANES), jnp.float32)
    bottom = [coef_ref[0, m, :total] for m in range(count)]
    lon = [coef_ref[1, m, :total] for m in range(count)]
    for m in range(count):
        cell_ref[0, m] = bottom[m]
        cell_ref[1, m] = jnp.minimum(bottom[m], east_of(bottom, m))
        cell_ref[2, m] = 0.5 * (lon[m] + east_of(lon, m))
        cell_ref[3, m] = jnp.minimum(bottom[m], coef_ref[0, m, 1 : total + 1])
        cell_ref[4, m] = 0.5 * (coef_ref[2, m, :total] + coef_ref[2, m, 1 : total + 1])


def gathered_phases(wide_ref, j, count, part):
    groups = wide_ref.shape[0]
    at = slice(j * SUB, (j + 1) * SUB)
    out = []
    for m in range(count):
        block, i = divmod(m, groups)
        which = part_of_lane(i * part, part, (SUB, LANES))
        x = wide_ref[groups - 1, block, at, :]
        for g in range(groups - 1):
            x = jnp.where(which == g, wide_ref[g, block, at, :], x)
        out.append(roll_lanes(x, -i * part))
    return out


def scattered_phases(xs, groups, part):
    out = [[] for _ in range(groups)]
    for first in range(0, len(xs), groups):
        turned = [roll_lanes(x, i * part) for i, x in enumerate(xs[first : first + groups])]
        for g in range(groups):
            which = part_of_lane(g * part, part, (SUB, LANES))
            x = turned[0]
            for i in range(1, len(turned)):
                x = jnp.where(which == i, turned[i], x)
            out[g].append(x)
    return out


def make_weights(part, level, scale, sigma, cell_ref, wide_ref, be_ref, bn_ref, root_ref, state_ref):
    total, count = be_ref.shape[:2]
    zero = jnp.zeros((SUB, LANES), jnp.float32)
    below, root_below = [zero] * count, [zero] * count
    skip = MARGIN - DEPTH
    for j in range(skip, total - skip):

        def spread(i, m):
            return jnp.broadcast_to(cell_ref[i, m, j : j + 1, :], (SUB, LANES))

        a_e = [jnp.where(level < spread(1, m), scale * spread(2, m), 0.0) for m in range(count)]
        a_n = [jnp.where(level < spread(3, m), scale * spread(4, m), 0.0) for m in range(count)]
        start = gathered_phases(wide_ref, j, count, part)
        root = []
        for m in range(count):
            d = 1.0 + a_e[m] + west_of(a_e, m) + a_n[m] + below[m]
            x = lax.rsqrt(d)
            x = x * (1.5 - 0.5 * d * x * x)
            root.append(x)
            root_ref[j, m] = x
            state_ref[j, m] = start[m] * jnp.where(level < spread(0, m), sigma * (d * x), 0.0)
        for m in range(count):
            be_ref[j, m] = a_e[m] * root[m] * east_of(root, m)
            bn_ref[j - 1, m] = below[m] * root_below[m] * root[m]
        below, root_below = a_n, root


def run_sweeps(first, last, count, be_ref, bn_ref, source_ref, state_ref):
    every = range(be_ref.shape[1])

    def sweep(_, carry):
        here = [state_ref[first, m] for m in every]
        south = [bn_ref[first - 1, m] * state_ref[first - 1, m] for m in every]
        for j in range(first, last):
            north = [state_ref[j + 1, m] for m in every]
            to_e = [be_ref[j, m] for m in every]
            to_n = [bn_ref[j, m] for m in every]
            flow = [to_e[m] * here[m] for m in every]
            for m in every:
                new = source_ref[j, m] + south[m] + to_n[m] * north[m]
                state_ref[j, m] = new + (to_e[m] * east_of(here, m) + west_of(flow, m))
            south = [to_n[m] * here[m] for m in every]
            here = north
        return carry

    lax.fori_loop(0, count, sweep, 0)


def sweep_kernel(coef_at, where_ref, scale_ref, sigma_ref, *refs):
    own_ref, west_ref, east_ref, south_ref, north_ref, whole_ref, part_ref = refs[:7]
    fine_ref, out_ref, window_ref, ghost_ref, wide_ref, coef_ref, cell_ref = refs[7:14]
    be_ref, bn_ref, root_ref, source_ref, state_ref, turn_ref = refs[14:20]
    phase_ref, plain_ref, mirror_ref = refs[20:]
    rows, padded, cols = own_ref.shape
    tiles, groups = cols // LANES, padded // SUB
    total, count = be_ref.shape[:2]
    part = layout(cols, groups)[1]
    body = MARGIN + rows
    skip = MARGIN - DEPTH
    is_top = where_ref[0]
    fill_tables(cols, where_ref, phase_ref, plain_ref, mirror_ref)

    def put(ref, j, pieces):
        for m, piece in enumerate(pieces):
            for g in range(groups):
                ref[g, m, j * SUB : (j + 1) * SUB] = piece[g * SUB : (g + 1) * SUB]

    def clear(ref, first, last):
        for j in range(first, last):
            put(ref, j, [jnp.zeros((padded, LANES), jnp.float32)] * ref.shape[1])

    clear(window_ref, 0, skip)
    for j in range(DEPTH):
        put(window_ref, skip + j, slab_row(south_ref, j, cols))
    lane = lane_iota((padded, LANES))
    for j in range(rows):
        v, s = divmod(j, PER)
        side = halo_lanes(west_ref[v], s * DEPTH, east_ref[v], s * DEPTH)
        side = jnp.where(lane < 2 * DEPTH, side, 0.0)
        put(
            window_ref,
            MARGIN + j,
            [own_ref[j, :, m * LANES : (m + 1) * LANES] for m in range(tiles)] + [side],
        )
    clear(ghost_ref, DEPTH, MARGIN)

    def widen(ref, used, matrix_ref, first):
        for g in range(groups):
            x = jnp.concatenate([ref[g, t] for t in range(used)], axis=1)
            wide = moved(x, matrix_ref[g], exact=g == groups - 1)
            for k in range(wide_ref.shape[1]):
                wide_ref[g, k, first : first + x.shape[0]] = wide[:, k * LANES : (k + 1) * LANES]

    @pl.when(is_top == 1)
    def _():
        for j in range(DEPTH):
            i = DEPTH - 1 - j
            put(ghost_ref, j, slab_row(whole_ref, i, cols) + [part_ref[i]])
        widen(ghost_ref, tiles + 2, mirror_ref, body * SUB)

    @pl.when(is_top == 0)
    def _():
        for j in range(DEPTH):
            put(ghost_ref, j, slab_row(north_ref, j, cols))
        widen(ghost_ref, tiles + 1, phase_ref, body * SUB)

    widen(window_ref, tiles + 1, phase_ref, 0)
    cell_terms(coef_at, part, wide_ref, coef_ref, cell_ref)

    c = lax.broadcasted_iota(jnp.int32, (SUB, LANES), 0) + lane_iota((SUB, LANES)) // part * SUB
    level = jnp.where(c < LEV, c, jnp.where(c < 2 * LEV, c - LEV, jnp.where(c == 2 * LEV, 0, LEV)))
    scale, sigma = (jnp.zeros((SUB, LANES), jnp.float32) for _ in range(2))
    for i in range(sigma_ref.shape[0]):
        scale = jnp.where(c == i, scale_ref[i], scale)
        sigma = jnp.where(c == i, sigma_ref[i], sigma)
    make_weights(
        part, level.astype(jnp.float32), scale, sigma, cell_ref, wide_ref, be_ref, bn_ref, root_ref, state_ref
    )

    done = 0
    for _step in range(STEPS):

        def make_source(j, carry):
            for m in range(count):
                root = root_ref[j, m]
                source_ref[j, m] = state_ref[j, m] * (root * root)
            return carry

        lax.fori_loop(skip + done, total - skip - done, make_source, 0, unroll=4)
        for some in (SWEEPS - SWEEPS // 2, SWEEPS // 2):
            if some > 0:
                run_sweeps(
                    skip + done + 1, total - skip - done - 1, some, be_ref, bn_ref, source_ref, state_ref
                )
            done += some

    for j in range(rows):
        at = MARGIN + j
        scaled = [state_ref[at, m] * (sigma * root_ref[at, m]) for m in range(count)]
        for g, pieces in enumerate(scattered_phases(scaled, groups, part)):
            for k, piece in enumerate(pieces):
                window_ref[g, k, j * SUB : (j + 1) * SUB] = piece
    for g in range(groups):
        x = jnp.concatenate(
            [window_ref[g, k, : rows * SUB] for k in range(wide_ref.shape[1])], axis=1
        )
        plain = moved(x, plain_ref[g]).reshape(rows, SUB, cols)
        fine_ref[:, g * SUB : (g + 1) * SUB, :] = plain
        for m in range(tiles):
            for j in range(rows):
                turn_ref[pl.ds(j, SUB, stride=rows), :] = plain[j, :, m * LANES : (m + 1) * LANES]
            for s in range(SUB):
                if g * SUB + s < out_ref.shape[0]:
                    out_ref[g * SUB + s, :, m * LANES : (m + 1) * LANES] = turn_ref[
                        s * rows : (s + 1) * rows, :
                    ]


def sweeps(where, own, around, length_scale, sigma, channels):
    rows, padded, cols = own.shape
    total = rows + 2 * MARGIN
    groups = padded // SUB
    count, _, blocks = layout(cols, groups)
    smem = pl.BlockSpec(memory_space=pltpu.SMEM)
    vmem = pl.BlockSpec(memory_space=pltpu.VMEM)
    plane = pltpu.VMEM((total, count, SUB, LANES), jnp.float32)
    tiles = max(cols // LANES + 1, blocks)
    return pl.pallas_call(
        functools.partial(sweep_kernel, channels % SUB),
        out_shape=(
            jax.ShapeDtypeStruct((rows, padded, cols), jnp.float32),
            jax.ShapeDtypeStruct((channels, rows, cols), jnp.float32),
        ),
        in_specs=[smem] * 3 + [vmem] * (1 + len(around)),
        out_specs=(vmem, vmem),
        scratch_shapes=[
            pltpu.VMEM((groups, tiles, (MARGIN + rows) * SUB, LANES), jnp.float32),
            pltpu.VMEM((groups, cols // LANES + 2, MARGIN * SUB, LANES), jnp.float32),
            pltpu.VMEM((groups, blocks, total * SUB, LANES), jnp.float32),
            pltpu.VMEM((COEFS, count, total + SUB, LANES), jnp.float32),
            pltpu.VMEM((5, count, total, LANES), jnp.float32),
        ]
        + [plane] * 5
        + [pltpu.VMEM((SUB * rows, LANES), jnp.float32)]
        + [
            pltpu.VMEM((groups, cols + LANES, blocks * LANES), jnp.bfloat16),
            pltpu.VMEM((groups, blocks * LANES, cols), jnp.bfloat16),
            pltpu.VMEM((groups, cols + 2 * LANES, blocks * LANES), jnp.bfloat16),
        ],
        compiler_params=params(28),
        name="sweeps",
    )(where, length_scale, sigma, own, *around)


def gather_kernel(channels, pair, fine_ref, obs_ref, out_ref, left_ref):
    senders, padded, slots = out_ref.shape
    rows, _, cols = fine_ref.shape
    high, low = split(fine_ref[...].reshape(rows * padded, cols))
    left_ref[:, :cols] = high
    left_ref[:, cols:] = low
    at_row, at_col = channels % SUB, (channels + 1) % SUB
    col_iota = lax.broadcasted_iota(jnp.int32, (cols, slots), 0).astype(jnp.float32)

    def body(step, carry):
        hots = []
        for s in range(pair):
            col = obs_ref[step * pair + s, at_col : at_col + 1, :]
            hots.append((col_iota == col).astype(jnp.bfloat16))
        hot = jnp.concatenate(hots, axis=1)
        found = jnp.dot(
            left_ref[...], jnp.concatenate([hot, hot], axis=0), preferred_element_type=jnp.float32
        )
        for s in range(pair):
            row = jnp.broadcast_to(obs_ref[step * pair + s, at_row : at_row + 1, :], (padded, slots))
            total = jnp.zeros((padded, slots), jnp.float32)
            for j in range(rows):
                piece = found[j * padded : (j + 1) * padded, s * slots : (s + 1) * slots]
                total = jnp.where(row == float(j), piece, total)
            out_ref[step * pair + s] = total
        return carry

    lax.fori_loop(0, senders // pair, body, 0)


def gather(fine, obs, channels):
    rows, padded, cols = fine.shape
    senders, _, slots = obs.shape
    pair = 2 if senders % 2 == 0 else 1
    where_group = channels // SUB
    vmem = pl.BlockSpec(memory_space=pltpu.VMEM)
    return pl.pallas_call(
        functools.partial(gather_kernel, channels, pair),
        grid=(1,),
        out_shape=jax.ShapeDtypeStruct((senders, padded, slots), jnp.float32),
        in_specs=[
            pl.BlockSpec((rows, padded, cols), lambda i: (0, 0, 0)),
            pl.BlockSpec((senders, SUB, slots), lambda i: (0, where_group, 0)),
        ],
        out_specs=pl.BlockSpec((senders, padded, slots), lambda i: (0, 0, 0)),
        scratch_shapes=[pltpu.VMEM((rows * padded, 2 * cols), jnp.bfloat16)],
        compiler_params=params(12),
        name="gather",
    )(fine, obs)


def per_device(
    obs_value, obs_cell, obs_count, bottom_level, diffusivity, partner, length_scale, sigma
):
    _, channels, owners, slots = obs_value.shape
    rows, cols = bottom_level.shape
    n_lat, n_lon = lax.axis_size("lat"), lax.axis_size("lon")
    padded = -(-(channels + COEFS) // SUB) * SUB
    vmem = pl.BlockSpec(memory_space=pltpu.VMEM)
    smem = pl.BlockSpec(memory_space=pltpu.SMEM)

    outgoing = pl.pallas_call(
        functools.partial(pack_kernel, channels, padded, cols),
        grid=(1,),
        out_shape=jax.ShapeDtypeStruct((owners * padded, slots), jnp.float32),
        in_specs=[
            smem,
            pl.BlockSpec((channels * owners, slots), lambda i: (0, 0)),
            pl.BlockSpec((owners, slots), lambda i: (0, 0)),
        ],
        out_specs=vmem,
        compiler_params=params(60),
        name="pack",
    )(obs_count, obs_value.reshape(channels * owners, slots), obs_cell[0])
    arrived = lax.all_to_all(
        outgoing.reshape(owners, padded, slots), ("lat", "lon"), split_axis=0, concat_axis=0, tiled=True
    )

    centre = lax.rem(partner[0] + lax.axis_index("lon") * cols, cols * n_lon)
    centre_col = centre % cols
    is_top = (lax.axis_index("lat") == n_lat - 1).astype(jnp.int32)
    kind = (centre_col >= cols // 2).astype(jnp.int32)
    where = jnp.stack([is_top, centre_col, kind])
    moves = Moves(n_lat, n_lon, centre // cols)

    own, west, east, *parts = scatter(arrived, bottom_level, diffusivity, channels)
    west, east = moves.east(east), moves.west(west)
    top, low = slabs(own, west, east)
    around = (west, east, *moves.slabs(kind, top, low, parts))
    fine, diffused = sweeps(where, own, around, length_scale, sigma, channels)
    local_fit = gather(fine, arrived, channels)
    returned = lax.all_to_all(local_fit, ("lat", "lon"), split_axis=0, concat_axis=0, tiled=True)
    obs_fit = pl.pallas_call(
        functools.partial(unpack_kernel, channels, padded),
        out_shape=jax.ShapeDtypeStruct((channels, owners, slots), jnp.float32),
        in_specs=[vmem],
        out_specs=vmem,
        compiler_params=params(),
        name="unpack",
    )(returned.reshape(owners * padded, slots))
    return obs_fit[None], diffused


def solution(mesh):
    return jax.shard_map(
        per_device,
        mesh=mesh,
        in_specs=(
            P(("lat", "lon"), None, None, None),
            P(("lat", "lon"), None, None),
            P(("lat", "lon"), None),
            P("lat", "lon"),
            P(None, "lat", "lon"),
            P("lon"),
            P(),
            P(),
        ),
        out_specs=(P(("lat", "lon"), None, None, None), P(None, "lat", "lon")),
        check_vma=False,
    )
```

```python
import functools

import jax
import jax.numpy as jnp
from jax import lax
from jax.experimental import pallas as pl
from jax.experimental.pallas import tpu as pltpu
from jax.sharding import PartitionSpec as P

LEV = 10
STEPS = 2
SWEEPS = 6
DEPTH = STEPS * SWEEPS
LANES = 128
SUB = 8
PER = LANES // DEPTH
MARGIN = -(-DEPTH // SUB) * SUB
COEFS = 3
MEGA = 1024 * 1024


def params(limit=8):
    return pltpu.CompilerParams(vmem_limit_bytes=limit * MEGA)


def lane_iota(shape):
    return lax.broadcasted_iota(jnp.int32, shape, len(shape) - 1)


def roll_lanes(x, shift):
    shift = shift % LANES
    return x if shift == 0 else pltpu.roll(x, shift, x.ndim - 1)


def pack_kernel(channels, padded, cols, count_ref, value_ref, cell_ref, out_ref):
    owners, slots = cell_ref.shape
    for c in range(channels):
        out_ref[pl.ds(c, owners, stride=padded), :] = value_ref[pl.ds(c * owners, owners), :]
    owner = lax.broadcasted_iota(jnp.int32, (owners, slots), 0)
    count = jnp.zeros((owners, slots), jnp.int32)
    for d in range(owners):
        count = jnp.where(owner == d, count_ref[0, d], count)
    cell = cell_ref[...].astype(jnp.float32)
    row = jnp.floor((cell + 0.5) * (1.0 / cols))
    col = cell - row * cols
    row = jnp.where(lane_iota((owners, slots)) < count, row, -1.0)
    out_ref[pl.ds(channels, owners, stride=padded), :] = row
    out_ref[pl.ds(channels + 1, owners, stride=padded), :] = col
    for c in range(channels + 2, padded):
        out_ref[pl.ds(c, owners, stride=padded), :] = jnp.zeros((owners, slots), jnp.float32)


def unpack_kernel(channels, padded, in_ref, out_ref):
    owners = out_ref.shape[1]
    for c in range(channels):
        out_ref[c] = in_ref[pl.ds(c, owners, stride=padded), :]


def layout(cols, groups):
    window = cols + 2 * DEPTH
    phases = -(-window // (LANES // groups))
    return phases, -(-window // phases), -(-phases // groups)


def split(x):
    high = x.astype(jnp.bfloat16)
    low = (x - high.astype(jnp.float32)).astype(jnp.bfloat16)
    return high, low


def turned_window(cols, groups, group, n):
    phases, part, _ = layout(cols, groups)
    block = n // LANES
    lane = lax.rem(n - block * LANES + (LANES - group * part % LANES), LANES)
    i = lane // part
    phase = block * groups + i
    return jnp.where((i < groups) & (phase < phases), (lane - i * part) * phases + phase, -1)


def window_source(cols, w):
    at = jnp.where(w < DEPTH, w + cols, jnp.where(w < DEPTH + cols, w - DEPTH, w))
    return jnp.where((w >= 0) & (w < cols + 2 * DEPTH), at, -1)


def moved(x, matrix, exact=False):
    dot = functools.partial(jnp.dot, preferred_element_type=jnp.float32)
    high, low = split(x)
    parts = [high, low]
    if exact:
        rest = (x - high.astype(jnp.float32)) - low.astype(jnp.float32)
        parts.append(rest.astype(jnp.bfloat16))
    return dot(jnp.concatenate(parts, axis=1), jnp.concatenate([matrix] * len(parts), axis=0))


def part_starts(cols):
    return DEPTH, cols - DEPTH - LANES


def mirror_source(cols, centre_col, kind, w):
    column = centre_col + DEPTH - w
    left, right = part_starts(cols)
    in_part = jnp.where(kind == 0, column - left, column + cols - right)
    in_whole = jnp.where(kind == 0, column + cols, column)
    at_whole = jnp.where(in_whole < 0, cols + DEPTH + in_whole, in_whole + jnp.where(in_whole < cols, 0, DEPTH))
    from_whole = (in_whole >= -DEPTH) & (in_whole < cols + DEPTH)
    at = jnp.where(from_whole, at_whole, cols + LANES + in_part)
    return jnp.where((w >= 0) & (w < cols + 2 * DEPTH), at, -1)


def fill_tables(cols, where_ref, phase_ref, plain_ref, mirror_ref):
    is_top, centre_col, kind = where_ref[0], where_ref[1], where_ref[2]
    groups = phase_ref.shape[0]
    phases, part, _ = layout(cols, groups)

    def lanes_of(ref):
        return lax.broadcasted_iota(jnp.int32, (1, ref.shape[-1]), 1)

    def hot(ref, at):
        source = lax.broadcasted_iota(jnp.int32, ref.shape[-2:], 0)
        return jnp.where(source == at, 1.0, 0.0).astype(jnp.bfloat16)

    for g in range(groups):
        w = turned_window(cols, groups, g, lanes_of(phase_ref))
        phase_ref[g] = hot(phase_ref, window_source(cols, w))
        w = lanes_of(plain_ref) + DEPTH
        phase, lane = w % phases, w // phases
        at = ((phase % groups + g) * part + lane) % LANES
        plain_ref[g] = hot(plain_ref, phase // groups * LANES + at)

    @pl.when(is_top == 1)
    def _():
        for g in range(groups):
            w = turned_window(cols, groups, g, lanes_of(mirror_ref))
            mirror_ref[g] = hot(mirror_ref, mirror_source(cols, centre_col, kind, w))


def strip_count(rows, width=DEPTH):
    return -(-rows // (LANES // width))


def pack_strip(read, count, first, out_ref):
    for v in range(out_ref.shape[0]):
        total = None
        for s in range(min(PER, count - v * PER)):
            x = roll_lanes(read(v * PER + s), s * DEPTH - first)
            total = x if total is None else jnp.where(lane_iota(x.shape) >= s * DEPTH, x, total)
        out_ref[v] = total


def halo_lanes(west, at_west, east, at_east, at=0):
    split_at = lane_iota(west.shape) < at + DEPTH
    return jnp.where(split_at, roll_lanes(west, at - at_west), roll_lanes(east, at + DEPTH - at_east))


def slab_kernel(own_ref, west_ref, east_ref, top_ref, low_ref):
    rows, _, cols = own_ref.shape
    tiles, per = cols // LANES, PER // 2
    for ref, first in ((top_ref, rows - DEPTH), (low_ref, 0)):
        for m in range(tiles):
            ref[m * DEPTH : (m + 1) * DEPTH] = own_ref[first : first + DEPTH, :, m * LANES : (m + 1) * LANES]
        for v in range(ref.shape[0] - tiles * DEPTH):
            total = None
            for s in range(min(per, DEPTH - v * per)):
                i, at = divmod(first + v * per + s, PER)
                x = halo_lanes(west_ref[i], at * DEPTH, east_ref[i], at * DEPTH, s * 2 * DEPTH)
                total = x if s == 0 else jnp.where(lane_iota(x.shape) >= s * 2 * DEPTH, x, total)
            ref[tiles * DEPTH + v] = total


def slabs(own, west, east):
    _, width, cols = own.shape
    count = cols // LANES * DEPTH + strip_count(DEPTH, 2 * DEPTH)
    vmem = pl.BlockSpec(memory_space=pltpu.VMEM)
    return pl.pallas_call(
        slab_kernel,
        out_shape=(jax.ShapeDtypeStruct((count, width, LANES), jnp.float32),) * 2,
        in_specs=[vmem] * 3,
        out_specs=(vmem,) * 2,
        compiler_params=params(),
        name="slabs",
    )(own, west, east)


class Moves:
    def __init__(self, n_lat, n_lon, centre_tile):
        self.to_east = [(i, (i + 1) % n_lon) for i in range(n_lon)]
        self.to_west = [(b, a) for a, b in self.to_east]
        self.to_north = [(i, i + 1) for i in range(n_lat - 1)]
        self.to_south = [(b, a) for a, b in self.to_north]
        self.n_lon = n_lon
        self.first = (n_lat - 1) * n_lon
        self.centre_tile = centre_tile

    def east(self, x):
        return lax.ppermute(x, "lon", self.to_east)

    def west(self, x):
        return lax.ppermute(x, "lon", self.to_west)

    def north(self, x):
        return lax.ppermute(x, "lat", self.to_north)

    def south(self, x):
        return lax.ppermute(x, "lat", self.to_south)

    def slabs(self, kind, top, low, parts):
        def pairs(tile, part):
            return [
                (self.first + s, self.first + (tile - part - s) % self.n_lon) for s in range(self.n_lon)
            ]

        def branch(tile, kind):
            def run(top, low, parts):
                part = lax.ppermute(parts[kind], ("lat", "lon"), pairs(tile, kind))
                part, slab = lax.optimization_barrier((part, top))
                whole = lax.ppermute(slab, ("lat", "lon"), pairs(tile, 1 - kind))
                return self.north(top), self.south(low), whole, part

            return run

        branches = [branch(t, k) for t in range(self.n_lon) for k in (0, 1)]
        return lax.switch(self.centre_tile * 2 + kind, branches, top, low, parts)


def scatter_kernel(channels, chunk, obs_ref, bottom_ref, kappa_ref, *refs):
    own_ref, west_ref, east_ref = refs[:3]
    part_refs, (left_ref, right_ref, sum_ref) = refs[3:5], refs[5:]
    senders, padded, slots = obs_ref.shape
    rows, _, cols = own_ref.shape
    row_iota = lax.broadcasted_iota(jnp.int32, (rows, slots), 0).astype(jnp.float32)
    col_iota = lax.broadcasted_iota(jnp.int32, (cols, slots), 0).astype(jnp.float32)

    def body(step, carry):
        for s in range(chunk):
            x = obs_ref[step * chunk + s]
            high, low = split(x)
            on_row = (row_iota == x[channels : channels + 1, :]).astype(jnp.bfloat16)
            on_col = (col_iota == x[channels + 1 : channels + 2, :]).astype(jnp.bfloat16)
            at = slice(s * slots, (s + 1) * slots)
            right_ref[:, at] = on_col
            for c in range(channels):
                left_ref[c * rows : (c + 1) * rows, at] = on_row * high[c : c + 1, :]
                left_ref[(channels + c) * rows : (channels + c + 1) * rows, at] = on_row * low[c : c + 1, :]
        part = lax.dot_general(
            left_ref[...], right_ref[...], (((1,), (1,)), ((), ())), preferred_element_type=jnp.float32
        )
        for m in range(cols // LANES):
            piece = part[:, m * LANES : (m + 1) * LANES]
            piece = piece[: channels * rows] + piece[channels * rows :]

            @pl.when(step == 0)
            def _():
                sum_ref[m, : channels * rows] = piece

            @pl.when(step > 0)
            def _():
                sum_ref[m, : channels * rows] += piece

        return carry

    lax.fori_loop(0, senders // chunk, body, 0)
    coefs = [bottom_ref[...].astype(jnp.float32), kappa_ref[0], kappa_ref[1]]
    for m in range(cols // LANES):
        at = slice(m * LANES, (m + 1) * LANES)
        for i, coef in enumerate(coefs):
            sum_ref[m, (channels + i) * rows : (channels + i + 1) * rows] = coef[:, at]
        for g in range(padded // SUB):
            for j in range(rows):
                own_ref[j, g * SUB : (g + 1) * SUB, at] = sum_ref[
                    m, pl.ds(g * SUB * rows + j, SUB, stride=rows), :
                ]
    pack_strip(lambda j: own_ref[j, :, :LANES], rows, 0, west_ref)
    pack_strip(lambda j: own_ref[j, :, cols - LANES :], rows, LANES - DEPTH, east_ref)
    for ref, start in zip(part_refs, part_starts(cols)):
        m, shift = divmod(start, LANES)
        for j in range(DEPTH):
            x = own_ref[rows - DEPTH + j, :, m * LANES : (m + 1) * LANES]
            y = own_ref[rows - DEPTH + j, :, (m + 1) * LANES : (m + 2) * LANES]
            here = lane_iota(x.shape) < LANES - shift
            ref[j] = jnp.where(here, roll_lanes(x, -shift), roll_lanes(y, -shift))


def scatter(obs, bottom_level, diffusivity, channels):
    senders, padded, slots = obs.shape
    rows, cols = bottom_level.shape
    tiles = cols // LANES
    chunk = 16 if senders % 16 == 0 else 1
    vmem = pl.BlockSpec(memory_space=pltpu.VMEM)
    side = (strip_count(rows), padded, LANES)
    part = (DEPTH, padded, LANES)
    shapes = [(rows, padded, cols), side, side, part, part]
    shapes = [jax.ShapeDtypeStruct(shape, jnp.float32) for shape in shapes]
    return pl.pallas_call(
        functools.partial(scatter_kernel, channels, chunk),
        out_shape=tuple(shapes),
        in_specs=[vmem] * 3,
        out_specs=(vmem,) * len(shapes),
        scratch_shapes=[
            pltpu.VMEM((2 * channels * rows, chunk * slots), jnp.bfloat16),
            pltpu.VMEM((cols, chunk * slots), jnp.bfloat16),
            pltpu.VMEM((tiles, padded * rows, LANES), jnp.float32),
        ],
        compiler_params=params(28),
        cost_estimate=pl.CostEstimate(
            flops=4 * senders * slots * padded * rows * cols, bytes_accessed=0, transcendentals=0
        ),
        name="scatter",
    )(obs, bottom_level, diffusivity)


def east_of(xs, m):
    return xs[m + 1] if m + 1 < len(xs) else roll_lanes(xs[0], -1)


def west_of(xs, m):
    return xs[m - 1] if m > 0 else roll_lanes(xs[-1], 1)


def slab_row(ref, j, cols):
    tiles, per = cols // LANES, PER // 2
    side = roll_lanes(ref[tiles * DEPTH + j // per], -(j % per) * 2 * DEPTH)
    side = jnp.where(lane_iota(side.shape) < 2 * DEPTH, side, 0.0)
    return [ref[m * DEPTH + j] for m in range(tiles)] + [side]


def part_of_lane(first, part, shape):
    return lax.rem(lane_iota(shape) + (LANES - first % LANES), LANES) // part


def cell_terms(coef_at, part, wide_ref, coef_ref, cell_ref):
    groups = wide_ref.shape[0]
    _, count, total, _ = cell_ref.shape
    which = part_of_lane(0, part, (total, LANES))
    for i in range(COEFS):
        for m in range(count):
            block, turn = divmod(m, groups)
            x = wide_ref[groups - 1, block, pl.ds(coef_at + i, total, stride=SUB), :]
            first = (groups - 1 + turn) * part
            out = jnp.zeros_like(x)
            for g in range(groups):
                out = jnp.where(which == g, roll_lanes(x, g * part - first), out)
            coef_ref[i, m, :total] = out
            coef_ref[i, m, total:] = jnp.zeros((SUB, LANES), jnp.float32)
    bottom = [coef_ref[0, m, :total] for m in range(count)]
    lon = [coef_ref[1, m, :total] for m in range(count)]
    for m in range(count):
        cell_ref[0, m] = bottom[m]
        cell_ref[1, m] = jnp.minimum(bottom[m], east_of(bottom, m))
        cell_ref[2, m] = 0.5 * (lon[m] + east_of(lon, m))
        cell_ref[3, m] = jnp.minimum(bottom[m], coef_ref[0, m, 1 : total + 1])
        cell_ref[4, m] = 0.5 * (coef_ref[2, m, :total] + coef_ref[2, m, 1 : total + 1])


def gathered_phases(wide_ref, j, count, part):
    groups = wide_ref.shape[0]
    at = slice(j * SUB, (j + 1) * SUB)
    out = []
    for m in range(count):
        block, i = divmod(m, groups)
        which = part_of_lane(i * part, part, (SUB, LANES))
        x = wide_ref[groups - 1, block, at, :]
        for g in range(groups - 1):
            x = jnp.where(which == g, wide_ref[g, block, at, :], x)
        out.append(roll_lanes(x, -i * part))
    return out


def scattered_phases(xs, groups, part):
    out = [[] for _ in range(groups)]
    for first in range(0, len(xs), groups):
        turned = [roll_lanes(x, i * part) for i, x in enumerate(xs[first : first + groups])]
        for g in range(groups):
            which = part_of_lane(g * part, part, (SUB, LANES))
            x = turned[0]
            for i in range(1, len(turned)):
                x = jnp.where(which == i, turned[i], x)
            out[g].append(x)
    return out


def make_weights(part, level, scale, sigma, cell_ref, wide_ref, be_ref, bn_ref, root_ref, state_ref):
    total, count = be_ref.shape[:2]
    zero = jnp.zeros((SUB, LANES), jnp.float32)
    below, root_below = [zero] * count, [zero] * count
    skip = MARGIN - DEPTH
    for j in range(skip, total - skip):

        def spread(i, m):
            return jnp.broadcast_to(cell_ref[i, m, j : j + 1, :], (SUB, LANES))

        a_e = [jnp.where(level < spread(1, m), scale * spread(2, m), 0.0) for m in range(count)]
        a_n = [jnp.where(level < spread(3, m), scale * spread(4, m), 0.0) for m in range(count)]
        start = gathered_phases(wide_ref, j, count, part)
        root = []
        for m in range(count):
            d = 1.0 + a_e[m] + west_of(a_e, m) + a_n[m] + below[m]
            x = lax.rsqrt(d)
            x = x * (1.5 - 0.5 * d * x * x)
            root.append(x)
            root_ref[j, m] = x
            state_ref[j, m] = start[m] * jnp.where(level < spread(0, m), sigma * (d * x), 0.0)
        for m in range(count):
            be_ref[j, m] = a_e[m] * root[m] * east_of(root, m)
            bn_ref[j - 1, m] = below[m] * root_below[m] * root[m]
        below, root_below = a_n, root


def run_sweeps(first, last, count, be_ref, bn_ref, source_ref, state_ref):
    every = range(be_ref.shape[1])

    def sweep(_, carry):
        here = [state_ref[first, m] for m in every]
        south = [bn_ref[first - 1, m] * state_ref[first - 1, m] for m in every]
        for j in range(first, last):
            north = [state_ref[j + 1, m] for m in every]
            to_e = [be_ref[j, m] for m in every]
            to_n = [bn_ref[j, m] for m in every]
            flow = [to_e[m] * here[m] for m in every]
            for m in every:
                new = source_ref[j, m] + south[m] + to_n[m] * north[m]
                state_ref[j, m] = new + (to_e[m] * east_of(here, m) + west_of(flow, m))
            south = [to_n[m] * here[m] for m in every]
            here = north
        return carry

    lax.fori_loop(0, count, sweep, 0)


def sweep_kernel(coef_at, where_ref, scale_ref, sigma_ref, *refs):
    own_ref, west_ref, east_ref = refs[:3]
    fine_ref, out_ref, window_ref, ghost_ref, wide_ref, coef_ref, cell_ref = refs[7:14]
    be_ref, bn_ref, root_ref, source_ref, state_ref, turn_ref = refs[14:20]
    phase_ref, plain_ref, mirror_ref = refs[20:23]
    south_ref, north_ref, whole_ref, part_ref = refs[23:27]
    copies = [
        pltpu.make_async_copy(source, target, refs[27].at[i])
        for i, (source, target) in enumerate(zip(refs[3:7], refs[23:27]))
    ]
    for copy in copies:
        copy.start()
    rows, padded, cols = own_ref.shape
    tiles, groups = cols // LANES, padded // SUB
    total, count = be_ref.shape[:2]
    part = layout(cols, groups)[1]
    body = MARGIN + rows
    skip = MARGIN - DEPTH
    is_top = where_ref[0]
    fill_tables(cols, where_ref, phase_ref, plain_ref, mirror_ref)

    def put(ref, j, pieces):
        for m, piece in enumerate(pieces):
            for g in range(groups):
                ref[g, m, j * SUB : (j + 1) * SUB] = piece[g * SUB : (g + 1) * SUB]

    def clear(ref, first, last):
        for j in range(first, last):
            put(ref, j, [jnp.zeros((padded, LANES), jnp.float32)] * ref.shape[1])

    clear(window_ref, 0, skip)
    lane = lane_iota((padded, LANES))
    for j in range(rows):
        v, s = divmod(j, PER)
        side = halo_lanes(west_ref[v], s * DEPTH, east_ref[v], s * DEPTH)
        side = jnp.where(lane < 2 * DEPTH, side, 0.0)
        put(
            window_ref,
            MARGIN + j,
            [own_ref[j, :, m * LANES : (m + 1) * LANES] for m in range(tiles)] + [side],
        )
    clear(ghost_ref, DEPTH, MARGIN)
    for copy in copies:
        copy.wait()
    for j in range(DEPTH):
        put(window_ref, skip + j, slab_row(south_ref, j, cols))

    def widen(ref, used, matrix_ref, first):
        for g in range(groups):
            x = jnp.concatenate([ref[g, t] for t in range(used)], axis=1)
            wide = moved(x, matrix_ref[g], exact=g == groups - 1)
            for k in range(wide_ref.shape[1]):
                wide_ref[g, k, first : first + x.shape[0]] = wide[:, k * LANES : (k + 1) * LANES]

    @pl.when(is_top == 1)
    def _():
        for j in range(DEPTH):
            i = DEPTH - 1 - j
            put(ghost_ref, j, slab_row(whole_ref, i, cols) + [part_ref[i]])
        widen(ghost_ref, tiles + 2, mirror_ref, body * SUB)

    @pl.when(is_top == 0)
    def _():
        for j in range(DEPTH):
            put(ghost_ref, j, slab_row(north_ref, j, cols))
        widen(ghost_ref, tiles + 1, phase_ref, body * SUB)

    widen(window_ref, tiles + 1, phase_ref, 0)
    cell_terms(coef_at, part, wide_ref, coef_ref, cell_ref)

    c = lax.broadcasted_iota(jnp.int32, (SUB, LANES), 0) + lane_iota((SUB, LANES)) // part * SUB
    level = jnp.where(c < LEV, c, jnp.where(c < 2 * LEV, c - LEV, jnp.where(c == 2 * LEV, 0, LEV)))
    scale, sigma = (jnp.zeros((SUB, LANES), jnp.float32) for _ in range(2))
    for i in range(sigma_ref.shape[0]):
        scale = jnp.where(c == i, scale_ref[i], scale)
        sigma = jnp.where(c == i, sigma_ref[i], sigma)
    make_weights(
        part, level.astype(jnp.float32), scale, sigma, cell_ref, wide_ref, be_ref, bn_ref, root_ref, state_ref
    )

    done = 0
    for _step in range(STEPS):

        def make_source(j, carry):
            for m in range(count):
                root = root_ref[j, m]
                source_ref[j, m] = state_ref[j, m] * (root * root)
            return carry

        lax.fori_loop(skip + done, total - skip - done, make_source, 0, unroll=4)
        for some in (SWEEPS - SWEEPS // 2, SWEEPS // 2):
            if some > 0:
                run_sweeps(
                    skip + done + 1, total - skip - done - 1, some, be_ref, bn_ref, source_ref, state_ref
                )
            done += some

    for j in range(rows):
        at = MARGIN + j
        scaled = [state_ref[at, m] * (sigma * root_ref[at, m]) for m in range(count)]
        for g, pieces in enumerate(scattered_phases(scaled, groups, part)):
            for k, piece in enumerate(pieces):
                window_ref[g, k, j * SUB : (j + 1) * SUB] = piece
    for g in range(groups):
        x = jnp.concatenate(
            [window_ref[g, k, : rows * SUB] for k in range(wide_ref.shape[1])], axis=1
        )
        plain = moved(x, plain_ref[g]).reshape(rows, SUB, cols)
        fine_ref[:, g * SUB : (g + 1) * SUB, :] = plain
        for m in range(tiles):
            for j in range(rows):
                turn_ref[pl.ds(j, SUB, stride=rows), :] = plain[j, :, m * LANES : (m + 1) * LANES]
            for s in range(SUB):
                if g * SUB + s < out_ref.shape[0]:
                    out_ref[g * SUB + s, :, m * LANES : (m + 1) * LANES] = turn_ref[
                        s * rows : (s + 1) * rows, :
                    ]


def sweeps(where, own, around, length_scale, sigma, channels):
    rows, padded, cols = own.shape
    total = rows + 2 * MARGIN
    groups = padded // SUB
    count, _, blocks = layout(cols, groups)
    smem = pl.BlockSpec(memory_space=pltpu.SMEM)
    vmem = pl.BlockSpec(memory_space=pltpu.VMEM)
    somewhere = pl.BlockSpec(memory_space=pl.ANY)
    plane = pltpu.VMEM((total, count, SUB, LANES), jnp.float32)
    late = around[2:]
    tiles = max(cols // LANES + 1, blocks)
    return pl.pallas_call(
        functools.partial(sweep_kernel, channels % SUB),
        out_shape=(
            jax.ShapeDtypeStruct((rows, padded, cols), jnp.float32),
            jax.ShapeDtypeStruct((channels, rows, cols), jnp.float32),
        ),
        in_specs=[smem] * 3 + [vmem] * 3 + [somewhere] * len(late),
        out_specs=(vmem, vmem),
        scratch_shapes=[
            pltpu.VMEM((groups, tiles, (MARGIN + rows) * SUB, LANES), jnp.float32),
            pltpu.VMEM((groups, cols // LANES + 2, MARGIN * SUB, LANES), jnp.float32),
            pltpu.VMEM((groups, blocks, total * SUB, LANES), jnp.float32),
            pltpu.VMEM((COEFS, count, total + SUB, LANES), jnp.float32),
            pltpu.VMEM((5, count, total, LANES), jnp.float32),
        ]
        + [plane] * 5
        + [pltpu.VMEM((SUB * rows, LANES), jnp.float32)]
        + [
            pltpu.VMEM((groups, cols + LANES, blocks * LANES), jnp.bfloat16),
            pltpu.VMEM((groups, blocks * LANES, cols), jnp.bfloat16),
            pltpu.VMEM((groups, cols + 2 * LANES, blocks * LANES), jnp.bfloat16),
        ]
        + [pltpu.VMEM(x.shape, jnp.float32) for x in late]
        + [pltpu.SemaphoreType.DMA((len(late),))],
        compiler_params=params(28),
        name="sweeps",
    )(where, length_scale, sigma, own, *around)


def gather_kernel(channels, pair, fine_ref, field_ref, obs_ref, out_ref, field_out_ref, left_ref, done_ref):
    copy = pltpu.make_async_copy(field_ref, field_out_ref, done_ref)
    copy.start()
    senders, padded, slots = out_ref.shape
    rows, _, cols = fine_ref.shape
    high, low = split(fine_ref[...].reshape(rows * padded, cols))
    left_ref[:, :cols] = high
    left_ref[:, cols:] = low
    at_row, at_col = channels, channels + 1
    col_iota = lax.broadcasted_iota(jnp.int32, (cols, slots), 0).astype(jnp.float32)

    def body(step, carry):
        hots = []
        for s in range(pair):
            col = obs_ref[step * pair + s, at_col : at_col + 1, :]
            hots.append((col_iota == col).astype(jnp.bfloat16))
        hot = jnp.concatenate(hots, axis=1)
        found = jnp.dot(
            left_ref[...], jnp.concatenate([hot, hot], axis=0), preferred_element_type=jnp.float32
        )
        for s in range(pair):
            row = jnp.broadcast_to(obs_ref[step * pair + s, at_row : at_row + 1, :], (SUB, slots))
            total = [jnp.zeros((SUB, slots), jnp.float32)] * (padded // SUB)
            for j in range(rows):
                here = row == float(j)
                for g in range(padded // SUB):
                    at = j * padded + g * SUB
                    piece = found[at : at + SUB, s * slots : (s + 1) * slots]
                    total[g] = jnp.where(here, piece, total[g])
            for g in range(padded // SUB):
                out_ref[step * pair + s, g * SUB : (g + 1) * SUB] = total[g]
        return carry

    lax.fori_loop(0, senders // pair, body, 0)
    copy.wait()


def gather(fine, field, obs, channels):
    rows, padded, cols = fine.shape
    senders, _, slots = obs.shape
    pair = 16 if senders % 16 == 0 else 1
    vmem = pl.BlockSpec(memory_space=pltpu.VMEM)
    return pl.pallas_call(
        functools.partial(gather_kernel, channels, pair),
        out_shape=(
            jax.ShapeDtypeStruct((senders, padded, slots), jnp.float32),
            jax.ShapeDtypeStruct(field.shape, jnp.float32),
        ),
        in_specs=[vmem] * 3,
        out_specs=(vmem, pl.BlockSpec(memory_space=pl.ANY)),
        scratch_shapes=[pltpu.VMEM((rows * padded, 2 * cols), jnp.bfloat16), pltpu.SemaphoreType.DMA],
        compiler_params=params(28),
        name="gather",
    )(fine, field, obs)


def per_device(
    obs_value, obs_cell, obs_count, bottom_level, diffusivity, partner, length_scale, sigma
):
    _, channels, owners, slots = obs_value.shape
    rows, cols = bottom_level.shape
    n_lat, n_lon = lax.axis_size("lat"), lax.axis_size("lon")
    padded = -(-(channels + COEFS) // SUB) * SUB
    vmem = pl.BlockSpec(memory_space=pltpu.VMEM)
    smem = pl.BlockSpec(memory_space=pltpu.SMEM)

    outgoing = pl.pallas_call(
        functools.partial(pack_kernel, channels, padded, cols),
        grid=(1,),
        out_shape=jax.ShapeDtypeStruct((owners * padded, slots), jnp.float32),
        in_specs=[
            smem,
            pl.BlockSpec((channels * owners, slots), lambda i: (0, 0)),
            pl.BlockSpec((owners, slots), lambda i: (0, 0)),
        ],
        out_specs=vmem,
        compiler_params=params(60),
        name="pack",
    )(obs_count, obs_value.reshape(channels * owners, slots), obs_cell[0])
    arrived = lax.all_to_all(
        outgoing.reshape(owners, padded, slots), ("lat", "lon"), split_axis=0, concat_axis=0, tiled=True
    )

    centre = lax.rem(partner[0] + lax.axis_index("lon") * cols, cols * n_lon)
    centre_col = centre % cols
    is_top = (lax.axis_index("lat") == n_lat - 1).astype(jnp.int32)
    kind = (centre_col >= cols // 2).astype(jnp.int32)
    where = jnp.stack([is_top, centre_col, kind])
    moves = Moves(n_lat, n_lon, centre // cols)

    own, west, east, *parts = scatter(arrived, bottom_level, diffusivity, channels)
    west, east = moves.east(east), moves.west(west)
    top, low = slabs(own, west, east)
    around = (west, east, *moves.slabs(kind, top, low, parts))
    fine, field = sweeps(where, own, around, length_scale, sigma, channels)
    local_fit, diffused = gather(fine, field, arrived, channels)
    returned = lax.all_to_all(local_fit, ("lat", "lon"), split_axis=0, concat_axis=0, tiled=True)
    obs_fit = pl.pallas_call(
        functools.partial(unpack_kernel, channels, padded),
        out_shape=jax.ShapeDtypeStruct((channels, owners, slots), jnp.float32),
        in_specs=[vmem],
        out_specs=vmem,
        compiler_params=params(),
        name="unpack",
    )(returned.reshape(owners * padded, slots))
    return obs_fit[None], diffused


def solution(mesh):
    return jax.shard_map(
        per_device,
        mesh=mesh,
        in_specs=(
            P(("lat", "lon"), None, None, None),
            P(("lat", "lon"), None, None),
            P(("lat", "lon"), None),
            P("lat", "lon"),
            P(None, "lat", "lon"),
            P("lon"),
            P(),
            P(),
        ),
        out_specs=(P(("lat", "lon"), None, None, None), P(None, "lat", "lon")),
        check_vma=False,
    )
```

```python
import functools

import jax
import jax.numpy as jnp
from jax import lax
from jax.experimental import pallas as pl
from jax.experimental.pallas import tpu as pltpu
from jax.sharding import PartitionSpec as P

LEV = 10
STEPS = 2
SWEEPS = 6
DEPTH = STEPS * SWEEPS
LANES = 128
SUB = 8
PER = LANES // DEPTH
MARGIN = -(-DEPTH // SUB) * SUB
COEFS = 3
MEGA = 1024 * 1024


def params(limit=8):
    return pltpu.CompilerParams(vmem_limit_bytes=limit * MEGA)


def lane_iota(shape):
    return lax.broadcasted_iota(jnp.int32, shape, len(shape) - 1)


def roll_lanes(x, shift):
    shift = shift % LANES
    return x if shift == 0 else pltpu.roll(x, shift, x.ndim - 1)


def pack_kernel(channels, width, cols, count_ref, value_ref, cell_ref, out_ref):
    owners, slots = cell_ref.shape
    for c in range(channels):
        out_ref[pl.ds(c, owners, stride=width), :] = value_ref[pl.ds(c * owners, owners), :]
    owner = lax.broadcasted_iota(jnp.int32, (owners, slots), 0)
    count = jnp.zeros((owners, slots), jnp.int32)
    for d in range(owners):
        count = jnp.where(owner == d, count_ref[0, d], count)
    cell = cell_ref[...].astype(jnp.float32)
    row = jnp.floor((cell + 0.5) * (1.0 / cols))
    col = cell - row * cols
    row = jnp.where(lane_iota((owners, slots)) < count, row, -1.0)
    out_ref[pl.ds(channels, owners, stride=width), :] = row
    out_ref[pl.ds(channels + 1, owners, stride=width), :] = col


def unpack_kernel(in_ref, out_ref):
    channels, owners, _ = out_ref.shape
    for c in range(channels):
        out_ref[c] = in_ref[pl.ds(c, owners, stride=channels), :]


def exchange(x, owners):
    rows, slots = x.shape
    x = x.reshape(owners, 1, rows // owners * slots)
    x = lax.all_to_all(x, ("lat", "lon"), split_axis=0, concat_axis=0, tiled=True)
    return x.reshape(rows, slots)


def layout(cols, groups):
    window = cols + 2 * DEPTH
    phases = -(-window // (LANES // groups))
    return phases, -(-window // phases), -(-phases // groups)


def split(x):
    high = x.astype(jnp.bfloat16)
    low = (x - high.astype(jnp.float32)).astype(jnp.bfloat16)
    return high, low


def turned_window(cols, groups, group, n):
    phases, part, _ = layout(cols, groups)
    block = n // LANES
    lane = lax.rem(n - block * LANES + (LANES - group * part % LANES), LANES)
    i = lane // part
    phase = block * groups + i
    return jnp.where((i < groups) & (phase < phases), (lane - i * part) * phases + phase, -1)


def window_source(cols, w):
    at = jnp.where(w < DEPTH, w + cols, jnp.where(w < DEPTH + cols, w - DEPTH, w))
    return jnp.where((w >= 0) & (w < cols + 2 * DEPTH), at, -1)


def moved(x, matrix, exact=False):
    dot = functools.partial(jnp.dot, preferred_element_type=jnp.float32)
    high, low = split(x)
    parts = [high, low]
    if exact:
        rest = (x - high.astype(jnp.float32)) - low.astype(jnp.float32)
        parts.append(rest.astype(jnp.bfloat16))
    return dot(jnp.concatenate(parts, axis=1), jnp.concatenate([matrix] * len(parts), axis=0))


def part_starts(cols):
    return DEPTH, cols - DEPTH - LANES


def mirror_source(cols, centre_col, kind, w):
    column = centre_col + DEPTH - w
    left, right = part_starts(cols)
    in_part = jnp.where(kind == 0, column - left, column + cols - right)
    in_whole = jnp.where(kind == 0, column + cols, column)
    at_whole = jnp.where(in_whole < 0, cols + DEPTH + in_whole, in_whole + jnp.where(in_whole < cols, 0, DEPTH))
    from_whole = (in_whole >= -DEPTH) & (in_whole < cols + DEPTH)
    at = jnp.where(from_whole, at_whole, cols + LANES + in_part)
    return jnp.where((w >= 0) & (w < cols + 2 * DEPTH), at, -1)


def fill_tables(cols, where_ref, phase_ref, plain_ref, mirror_ref):
    is_top, centre_col, kind = where_ref[0], where_ref[1], where_ref[2]
    groups = phase_ref.shape[0]
    phases, part, _ = layout(cols, groups)

    def lanes_of(ref):
        return lax.broadcasted_iota(jnp.int32, (1, ref.shape[-1]), 1)

    def hot(ref, at):
        source = lax.broadcasted_iota(jnp.int32, ref.shape[-2:], 0)
        return jnp.where(source == at, 1.0, 0.0).astype(jnp.bfloat16)

    for g in range(groups):
        w = turned_window(cols, groups, g, lanes_of(phase_ref))
        phase_ref[g] = hot(phase_ref, window_source(cols, w))
        w = lanes_of(plain_ref) + DEPTH
        phase, lane = w % phases, w // phases
        at = ((phase % groups + g) * part + lane) % LANES
        plain_ref[g] = hot(plain_ref, phase // groups * LANES + at)

    @pl.when(is_top == 1)
    def _():
        for g in range(groups):
            w = turned_window(cols, groups, g, lanes_of(mirror_ref))
            mirror_ref[g] = hot(mirror_ref, mirror_source(cols, centre_col, kind, w))


def strip_count(rows, width=DEPTH):
    return -(-rows // (LANES // width))


def pack_strip(read, count, first, out_ref):
    for v in range(out_ref.shape[0]):
        total = None
        for s in range(min(PER, count - v * PER)):
            x = roll_lanes(read(v * PER + s), s * DEPTH - first)
            total = x if total is None else jnp.where(lane_iota(x.shape) >= s * DEPTH, x, total)
        out_ref[v] = total


def halo_lanes(west, at_west, east, at_east, at=0):
    split_at = lane_iota(west.shape) < at + DEPTH
    return jnp.where(split_at, roll_lanes(west, at - at_west), roll_lanes(east, at + DEPTH - at_east))


def slab_kernel(own_ref, west_ref, east_ref, top_ref, low_ref):
    rows, _, cols = own_ref.shape
    tiles, per = cols // LANES, PER // 2
    for ref, first in ((top_ref, rows - DEPTH), (low_ref, 0)):
        for m in range(tiles):
            ref[m * DEPTH : (m + 1) * DEPTH] = own_ref[first : first + DEPTH, :, m * LANES : (m + 1) * LANES]
        for v in range(ref.shape[0] - tiles * DEPTH):
            total = None
            for s in range(min(per, DEPTH - v * per)):
                i, at = divmod(first + v * per + s, PER)
                x = halo_lanes(west_ref[i], at * DEPTH, east_ref[i], at * DEPTH, s * 2 * DEPTH)
                total = x if s == 0 else jnp.where(lane_iota(x.shape) >= s * 2 * DEPTH, x, total)
            ref[tiles * DEPTH + v] = total


def slabs(own, west, east):
    _, width, cols = own.shape
    count = cols // LANES * DEPTH + strip_count(DEPTH, 2 * DEPTH)
    vmem = pl.BlockSpec(memory_space=pltpu.VMEM)
    return pl.pallas_call(
        slab_kernel,
        out_shape=(jax.ShapeDtypeStruct((count, width, LANES), jnp.float32),) * 2,
        in_specs=[vmem] * 3,
        out_specs=(vmem,) * 2,
        compiler_params=params(),
        name="slabs",
    )(own, west, east)


class Moves:
    def __init__(self, n_lat, n_lon, centre_tile):
        self.to_east = [(i, (i + 1) % n_lon) for i in range(n_lon)]
        self.to_west = [(b, a) for a, b in self.to_east]
        self.to_north = [(i, i + 1) for i in range(n_lat - 1)]
        self.to_south = [(b, a) for a, b in self.to_north]
        self.n_lon = n_lon
        self.first = (n_lat - 1) * n_lon
        self.centre_tile = centre_tile

    def east(self, x):
        return lax.ppermute(x, "lon", self.to_east)

    def west(self, x):
        return lax.ppermute(x, "lon", self.to_west)

    def north(self, x):
        return lax.ppermute(x, "lat", self.to_north)

    def south(self, x):
        return lax.ppermute(x, "lat", self.to_south)

    def fold(self, part, send, *operands):
        first, n = self.first, self.n_lon

        def branch(tile):
            pairs = [(first + s, first + (tile - s) % n) for s in range(n)]
            return lambda *xs: send(lambda x: lax.ppermute(x, ("lat", "lon"), pairs), *xs)

        tile = lax.rem(self.centre_tile + n - part, n)
        return lax.switch(tile, [branch(t) for t in range(n)], *operands)


def scatter_kernel(channels, chunk, where_ref, obs_ref, bottom_ref, kappa_ref, *refs):
    own_ref, west_ref, east_ref = refs[:3]
    part_ref, left_ref, right_ref, sum_ref, blocks_ref = refs[3:]
    rows, padded, cols = own_ref.shape
    slots = obs_ref.shape[1]
    senders = blocks_ref.shape[0] // padded
    for c in range(channels + 2):
        blocks_ref[pl.ds(c, senders, stride=padded), :] = obs_ref[pl.ds(c, senders, stride=channels + 2), :]
    row_iota = lax.broadcasted_iota(jnp.int32, (rows, slots), 0).astype(jnp.float32)
    col_iota = lax.broadcasted_iota(jnp.int32, (cols, slots), 0).astype(jnp.float32)

    def body(step, carry):
        for s in range(chunk):
            at = pl.multiple_of((step * chunk + s) * padded, SUB)
            x = blocks_ref[pl.ds(at, padded), :]
            high, low = split(x)
            on_row = (row_iota == x[channels : channels + 1, :]).astype(jnp.bfloat16)
            on_col = (col_iota == x[channels + 1 : channels + 2, :]).astype(jnp.bfloat16)
            at = slice(s * slots, (s + 1) * slots)
            right_ref[:, at] = on_col
            for c in range(channels):
                left_ref[c * rows : (c + 1) * rows, at] = on_row * high[c : c + 1, :]
                left_ref[(channels + c) * rows : (channels + c + 1) * rows, at] = on_row * low[c : c + 1, :]
        part = lax.dot_general(
            left_ref[...], right_ref[...], (((1,), (1,)), ((), ())), preferred_element_type=jnp.float32
        )
        for m in range(cols // LANES):
            piece = part[:, m * LANES : (m + 1) * LANES]
            piece = piece[: channels * rows] + piece[channels * rows :]

            @pl.when(step == 0)
            def _():
                sum_ref[m, : channels * rows] = piece

            @pl.when(step > 0)
            def _():
                sum_ref[m, : channels * rows] += piece

        return carry

    lax.fori_loop(0, senders // chunk, body, 0)
    coefs = [bottom_ref[...].astype(jnp.float32), kappa_ref[0], kappa_ref[1]]
    for m in range(cols // LANES):
        at = slice(m * LANES, (m + 1) * LANES)
        for i, coef in enumerate(coefs):
            sum_ref[m, (channels + i) * rows : (channels + i + 1) * rows] = coef[:, at]
        for g in range(padded // SUB):
            for j in range(rows):
                own_ref[j, g * SUB : (g + 1) * SUB, at] = sum_ref[
                    m, pl.ds(g * SUB * rows + j, SUB, stride=rows), :
                ]
    pack_strip(lambda j: own_ref[j, :, :LANES], rows, 0, west_ref)
    pack_strip(lambda j: own_ref[j, :, cols - LANES :], rows, LANES - DEPTH, east_ref)
    for kind, start in enumerate(part_starts(cols)):

        @pl.when(where_ref[2] == kind)
        def _():
            m, shift = divmod(start, LANES)
            for j in range(DEPTH):
                x = own_ref[rows - DEPTH + j, :, m * LANES : (m + 1) * LANES]
                y = own_ref[rows - DEPTH + j, :, (m + 1) * LANES : (m + 2) * LANES]
                here = lane_iota(x.shape) < LANES - shift
                part_ref[j] = jnp.where(here, roll_lanes(x, -shift), roll_lanes(y, -shift))


def scatter(where, obs, bottom_level, diffusivity, channels, padded):
    slots = obs.shape[1]
    senders = obs.shape[0] // (channels + 2)
    rows, cols = bottom_level.shape
    tiles = cols // LANES
    chunk = 16 if senders % 16 == 0 else 1
    vmem = pl.BlockSpec(memory_space=pltpu.VMEM)
    side = (strip_count(rows), padded, LANES)
    part = (DEPTH, padded, LANES)
    shapes = [(rows, padded, cols), side, side, part]
    shapes = [jax.ShapeDtypeStruct(shape, jnp.float32) for shape in shapes]
    return pl.pallas_call(
        functools.partial(scatter_kernel, channels, chunk),
        out_shape=tuple(shapes),
        in_specs=[pl.BlockSpec(memory_space=pltpu.SMEM)] + [vmem] * 3,
        out_specs=(vmem,) * len(shapes),
        scratch_shapes=[
            pltpu.VMEM((2 * channels * rows, chunk * slots), jnp.bfloat16),
            pltpu.VMEM((cols, chunk * slots), jnp.bfloat16),
            pltpu.VMEM((tiles, padded * rows, LANES), jnp.float32),
            pltpu.VMEM((senders * padded, slots), jnp.float32),
        ],
        compiler_params=params(28),
        cost_estimate=pl.CostEstimate(
            flops=4 * senders * slots * padded * rows * cols, bytes_accessed=0, transcendentals=0
        ),
        name="scatter",
    )(where, obs, bottom_level, diffusivity)


def east_of(xs, m):
    return xs[m + 1] if m + 1 < len(xs) else roll_lanes(xs[0], -1)


def west_of(xs, m):
    return xs[m - 1] if m > 0 else roll_lanes(xs[-1], 1)


def slab_row(ref, j, cols):
    tiles, per = cols // LANES, PER // 2
    side = roll_lanes(ref[tiles * DEPTH + j // per], -(j % per) * 2 * DEPTH)
    side = jnp.where(lane_iota(side.shape) < 2 * DEPTH, side, 0.0)
    return [ref[m * DEPTH + j] for m in range(tiles)] + [side]


def part_of_lane(first, part, shape):
    return lax.rem(lane_iota(shape) + (LANES - first % LANES), LANES) // part


def cell_terms(coef_at, part, wide_ref, coef_ref, cell_ref):
    groups = wide_ref.shape[0]
    _, count, total, _ = cell_ref.shape
    which = part_of_lane(0, part, (total, LANES))
    for i in range(COEFS):
        for m in range(count):
            block, turn = divmod(m, groups)
            x = wide_ref[groups - 1, block, pl.ds(coef_at + i, total, stride=SUB), :]
            first = (groups - 1 + turn) * part
            out = jnp.zeros_like(x)
            for g in range(groups):
                out = jnp.where(which == g, roll_lanes(x, g * part - first), out)
            coef_ref[i, m, :total] = out
            coef_ref[i, m, total:] = jnp.zeros((SUB, LANES), jnp.float32)
    bottom = [coef_ref[0, m, :total] for m in range(count)]
    lon = [coef_ref[1, m, :total] for m in range(count)]
    for m in range(count):
        cell_ref[0, m] = bottom[m]
        cell_ref[1, m] = jnp.minimum(bottom[m], east_of(bottom, m))
        cell_ref[2, m] = 0.5 * (lon[m] + east_of(lon, m))
        cell_ref[3, m] = jnp.minimum(bottom[m], coef_ref[0, m, 1 : total + 1])
        cell_ref[4, m] = 0.5 * (coef_ref[2, m, :total] + coef_ref[2, m, 1 : total + 1])


def gathered_phases(wide_ref, j, count, part):
    groups = wide_ref.shape[0]
    at = slice(j * SUB, (j + 1) * SUB)
    out = []
    for m in range(count):
        block, i = divmod(m, groups)
        which = part_of_lane(i * part, part, (SUB, LANES))
        x = wide_ref[groups - 1, block, at, :]
        for g in range(groups - 1):
            x = jnp.where(which == g, wide_ref[g, block, at, :], x)
        out.append(roll_lanes(x, -i * part))
    return out


def scattered_phases(xs, groups, part):
    out = [[] for _ in range(groups)]
    for first in range(0, len(xs), groups):
        turned = [roll_lanes(x, i * part) for i, x in enumerate(xs[first : first + groups])]
        for g in range(groups):
            which = part_of_lane(g * part, part, (SUB, LANES))
            x = turned[0]
            for i in range(1, len(turned)):
                x = jnp.where(which == i, turned[i], x)
            out[g].append(x)
    return out


def make_weights(part, level, scale, sigma, cell_ref, wide_ref, be_ref, bn_ref, root_ref, state_ref):
    total, count = be_ref.shape[:2]
    zero = jnp.zeros((SUB, LANES), jnp.float32)
    below, root_below = [zero] * count, [zero] * count
    skip = MARGIN - DEPTH
    for j in range(skip, total - skip):

        def spread(i, m):
            return jnp.broadcast_to(cell_ref[i, m, j : j + 1, :], (SUB, LANES))

        a_e = [jnp.where(level < spread(1, m), scale * spread(2, m), 0.0) for m in range(count)]
        a_n = [jnp.where(level < spread(3, m), scale * spread(4, m), 0.0) for m in range(count)]
        start = gathered_phases(wide_ref, j, count, part)
        root = []
        for m in range(count):
            d = 1.0 + a_e[m] + west_of(a_e, m) + a_n[m] + below[m]
            x = lax.rsqrt(d)
            x = x * (1.5 - 0.5 * d * x * x)
            root.append(x)
            root_ref[j, m] = x
            state_ref[j, m] = start[m] * jnp.where(level < spread(0, m), sigma * (d * x), 0.0)
        for m in range(count):
            be_ref[j, m] = a_e[m] * root[m] * east_of(root, m)
            bn_ref[j - 1, m] = below[m] * root_below[m] * root[m]
        below, root_below = a_n, root


def run_sweeps(first, last, count, be_ref, bn_ref, source_ref, state_ref):
    every = range(be_ref.shape[1])

    def sweep(_, carry):
        here = [state_ref[first, m] for m in every]
        south = [bn_ref[first - 1, m] * state_ref[first - 1, m] for m in every]
        for j in range(first, last):
            north = [state_ref[j + 1, m] for m in every]
            to_e = [be_ref[j, m] for m in every]
            to_n = [bn_ref[j, m] for m in every]
            flow = [to_e[m] * here[m] for m in every]
            for m in every:
                new = source_ref[j, m] + south[m] + to_n[m] * north[m]
                state_ref[j, m] = new + (to_e[m] * east_of(here, m) + west_of(flow, m))
            south = [to_n[m] * here[m] for m in every]
            here = north
        return carry

    lax.fori_loop(0, count, sweep, 0)


def sweep_kernel(coef_at, where_ref, scale_ref, sigma_ref, *refs):
    own_ref, west_ref, east_ref = refs[:3]
    fine_ref, out_ref, window_ref, ghost_ref, wide_ref, coef_ref, cell_ref = refs[7:14]
    be_ref, bn_ref, root_ref, source_ref, state_ref, turn_ref = refs[14:20]
    phase_ref, plain_ref, mirror_ref = refs[20:23]
    south_ref, north_ref, whole_ref, part_ref = refs[23:27]
    copies = [
        pltpu.make_async_copy(source, target, refs[27].at[i])
        for i, (source, target) in enumerate(zip(refs[3:7], refs[23:27]))
    ]
    for copy in copies:
        copy.start()
    rows, padded, cols = own_ref.shape
    tiles, groups = cols // LANES, padded // SUB
    total, count = be_ref.shape[:2]
    part = layout(cols, groups)[1]
    body = MARGIN + rows
    skip = MARGIN - DEPTH
    is_top = where_ref[0]
    fill_tables(cols, where_ref, phase_ref, plain_ref, mirror_ref)

    def put(ref, j, pieces):
        for m, piece in enumerate(pieces):
            for g in range(groups):
                ref[g, m, j * SUB : (j + 1) * SUB] = piece[g * SUB : (g + 1) * SUB]

    def clear(ref, first, last):
        for j in range(first, last):
            put(ref, j, [jnp.zeros((padded, LANES), jnp.float32)] * ref.shape[1])

    clear(window_ref, 0, skip)
    lane = lane_iota((padded, LANES))
    for j in range(rows):
        v, s = divmod(j, PER)
        side = halo_lanes(west_ref[v], s * DEPTH, east_ref[v], s * DEPTH)
        side = jnp.where(lane < 2 * DEPTH, side, 0.0)
        put(
            window_ref,
            MARGIN + j,
            [own_ref[j, :, m * LANES : (m + 1) * LANES] for m in range(tiles)] + [side],
        )
    clear(ghost_ref, DEPTH, MARGIN)
    for copy in copies:
        copy.wait()
    for j in range(DEPTH):
        put(window_ref, skip + j, slab_row(south_ref, j, cols))

    def widen(ref, used, matrix_ref, first):
        for g in range(groups):
            x = jnp.concatenate([ref[g, t] for t in range(used)], axis=1)
            wide = moved(x, matrix_ref[g], exact=g == groups - 1)
            for k in range(wide_ref.shape[1]):
                wide_ref[g, k, first : first + x.shape[0]] = wide[:, k * LANES : (k + 1) * LANES]

    @pl.when(is_top == 1)
    def _():
        for j in range(DEPTH):
            i = DEPTH - 1 - j
            put(ghost_ref, j, slab_row(whole_ref, i, cols) + [part_ref[i]])
        widen(ghost_ref, tiles + 2, mirror_ref, body * SUB)

    @pl.when(is_top == 0)
    def _():
        for j in range(DEPTH):
            put(ghost_ref, j, slab_row(north_ref, j, cols))
        widen(ghost_ref, tiles + 1, phase_ref, body * SUB)

    widen(window_ref, tiles + 1, phase_ref, 0)
    cell_terms(coef_at, part, wide_ref, coef_ref, cell_ref)

    c = lax.broadcasted_iota(jnp.int32, (SUB, LANES), 0) + lane_iota((SUB, LANES)) // part * SUB
    level = jnp.where(c < LEV, c, jnp.where(c < 2 * LEV, c - LEV, jnp.where(c == 2 * LEV, 0, LEV)))
    scale, sigma = (jnp.zeros((SUB, LANES), jnp.float32) for _ in range(2))
    for i in range(sigma_ref.shape[0]):
        scale = jnp.where(c == i, scale_ref[i], scale)
        sigma = jnp.where(c == i, sigma_ref[i], sigma)
    make_weights(
        part, level.astype(jnp.float32), scale, sigma, cell_ref, wide_ref, be_ref, bn_ref, root_ref, state_ref
    )

    done = 0
    for _step in range(STEPS):

        def make_source(j, carry):
            for m in range(count):
                root = root_ref[j, m]
                source_ref[j, m] = state_ref[j, m] * (root * root)
            return carry

        lax.fori_loop(skip + done, total - skip - done, make_source, 0, unroll=4)
        for some in (SWEEPS - SWEEPS // 2, SWEEPS // 2):
            if some > 0:
                run_sweeps(
                    skip + done + 1, total - skip - done - 1, some, be_ref, bn_ref, source_ref, state_ref
                )
            done += some

    for j in range(rows):
        at = MARGIN + j
        scaled = [state_ref[at, m] * (sigma * root_ref[at, m]) for m in range(count)]
        for g, pieces in enumerate(scattered_phases(scaled, groups, part)):
            for k, piece in enumerate(pieces):
                window_ref[g, k, j * SUB : (j + 1) * SUB] = piece
    for g in range(groups):
        x = jnp.concatenate(
            [window_ref[g, k, : rows * SUB] for k in range(wide_ref.shape[1])], axis=1
        )
        plain = moved(x, plain_ref[g]).reshape(rows, SUB, cols)
        fine_ref[:, g * SUB : (g + 1) * SUB, :] = plain
        for m in range(tiles):
            for j in range(rows):
                turn_ref[pl.ds(j, SUB, stride=rows), :] = plain[j, :, m * LANES : (m + 1) * LANES]
            for s in range(SUB):
                if g * SUB + s < out_ref.shape[0]:
                    out_ref[g * SUB + s, :, m * LANES : (m + 1) * LANES] = turn_ref[
                        s * rows : (s + 1) * rows, :
                    ]


def sweeps(where, own, around, length_scale, sigma, channels):
    rows, padded, cols = own.shape
    total = rows + 2 * MARGIN
    groups = padded // SUB
    count, _, blocks = layout(cols, groups)
    smem = pl.BlockSpec(memory_space=pltpu.SMEM)
    vmem = pl.BlockSpec(memory_space=pltpu.VMEM)
    somewhere = pl.BlockSpec(memory_space=pl.ANY)
    plane = pltpu.VMEM((total, count, SUB, LANES), jnp.float32)
    late = around[2:]
    tiles = max(cols // LANES + 1, blocks)
    return pl.pallas_call(
        functools.partial(sweep_kernel, channels % SUB),
        out_shape=(
            jax.ShapeDtypeStruct((rows, padded, cols), jnp.float32),
            jax.ShapeDtypeStruct((channels, rows, cols), jnp.float32),
        ),
        in_specs=[smem] * 3 + [vmem] * 3 + [somewhere] * len(late),
        out_specs=(vmem, vmem),
        scratch_shapes=[
            pltpu.VMEM((groups, tiles, (MARGIN + rows) * SUB, LANES), jnp.float32),
            pltpu.VMEM((groups, cols // LANES + 2, MARGIN * SUB, LANES), jnp.float32),
            pltpu.VMEM((groups, blocks, total * SUB, LANES), jnp.float32),
            pltpu.VMEM((COEFS, count, total + SUB, LANES), jnp.float32),
            pltpu.VMEM((5, count, total, LANES), jnp.float32),
        ]
        + [plane] * 5
        + [pltpu.VMEM((SUB * rows, LANES), jnp.float32)]
        + [
            pltpu.VMEM((groups, cols + LANES, blocks * LANES), jnp.bfloat16),
            pltpu.VMEM((groups, blocks * LANES, cols), jnp.bfloat16),
            pltpu.VMEM((groups, cols + 2 * LANES, blocks * LANES), jnp.bfloat16),
        ]
        + [pltpu.VMEM(x.shape, jnp.float32) for x in late]
        + [pltpu.SemaphoreType.DMA((len(late),))],
        compiler_params=params(28),
        name="sweeps",
    )(where, length_scale, sigma, own, *around)


def gather_kernel(channels, pair, fine_ref, field_ref, obs_ref, out_ref, field_out_ref, *scratch):
    left_ref, cells_ref, blocks_ref, done_ref = scratch
    copy = pltpu.make_async_copy(field_ref, field_out_ref, done_ref)
    copy.start()
    rows, padded, cols = fine_ref.shape
    slots = obs_ref.shape[1]
    senders = blocks_ref.shape[0] // padded
    for i in (0, 1):
        cells_ref[pl.ds(i, senders, stride=SUB), :] = obs_ref[
            pl.ds(channels + i, senders, stride=channels + 2), :
        ]
    high, low = split(fine_ref[...].reshape(rows * padded, cols))
    left_ref[:, :cols] = high
    left_ref[:, cols:] = low
    col_iota = lax.broadcasted_iota(jnp.int32, (cols, slots), 0).astype(jnp.float32)

    def body(step, carry):
        hots = []
        for s in range(pair):
            col = cells_ref[pl.ds(pl.multiple_of((step * pair + s) * SUB, SUB), SUB), :][1:2, :]
            hots.append((col_iota == col).astype(jnp.bfloat16))
        hot = jnp.concatenate(hots, axis=1)
        found = jnp.dot(
            left_ref[...], jnp.concatenate([hot, hot], axis=0), preferred_element_type=jnp.float32
        )
        for s in range(pair):
            row = cells_ref[pl.ds(pl.multiple_of((step * pair + s) * SUB, SUB), SUB), :][:1, :]
            row = jnp.broadcast_to(row, (SUB, slots))
            total = [jnp.zeros((SUB, slots), jnp.float32)] * (padded // SUB)
            for j in range(rows):
                here = row == float(j)
                for g in range(padded // SUB):
                    at = j * padded + g * SUB
                    piece = found[at : at + SUB, s * slots : (s + 1) * slots]
                    total[g] = jnp.where(here, piece, total[g])
            for g in range(padded // SUB):
                at = pl.multiple_of((step * pair + s) * padded + g * SUB, SUB)
                blocks_ref[pl.ds(at, SUB), :] = total[g]
        return carry

    lax.fori_loop(0, senders // pair, body, 0)
    for c in range(channels):
        out_ref[pl.ds(c, senders, stride=channels), :] = blocks_ref[pl.ds(c, senders, stride=padded), :]
    copy.wait()


def gather(fine, field, obs, channels):
    rows, padded, cols = fine.shape
    slots = obs.shape[1]
    senders = obs.shape[0] // (channels + 2)
    pair = 16 if senders % 16 == 0 else 1
    vmem = pl.BlockSpec(memory_space=pltpu.VMEM)
    return pl.pallas_call(
        functools.partial(gather_kernel, channels, pair),
        out_shape=(
            jax.ShapeDtypeStruct((senders * channels, slots), jnp.float32),
            jax.ShapeDtypeStruct(field.shape, jnp.float32),
        ),
        in_specs=[vmem] * 3,
        out_specs=(vmem, pl.BlockSpec(memory_space=pl.ANY)),
        scratch_shapes=[
            pltpu.VMEM((rows * padded, 2 * cols), jnp.bfloat16),
            pltpu.VMEM((senders * SUB, slots), jnp.float32),
            pltpu.VMEM((senders * padded, slots), jnp.float32),
            pltpu.SemaphoreType.DMA,
        ],
        compiler_params=params(28),
        name="gather",
    )(fine, field, obs)


def per_device(
    obs_value, obs_cell, obs_count, bottom_level, diffusivity, partner, length_scale, sigma
):
    _, channels, owners, slots = obs_value.shape
    rows, cols = bottom_level.shape
    n_lat, n_lon = lax.axis_size("lat"), lax.axis_size("lon")
    padded = -(-(channels + COEFS) // SUB) * SUB
    vmem = pl.BlockSpec(memory_space=pltpu.VMEM)
    smem = pl.BlockSpec(memory_space=pltpu.SMEM)

    outgoing = pl.pallas_call(
        functools.partial(pack_kernel, channels, channels + 2, cols),
        grid=(1,),
        out_shape=jax.ShapeDtypeStruct((owners * (channels + 2), slots), jnp.float32),
        in_specs=[
            smem,
            pl.BlockSpec((channels * owners, slots), lambda i: (0, 0)),
            pl.BlockSpec((owners, slots), lambda i: (0, 0)),
        ],
        out_specs=vmem,
        compiler_params=params(60),
        name="pack",
    )(obs_count, obs_value.reshape(channels * owners, slots), obs_cell[0])
    arrived = exchange(outgoing, owners)

    centre = lax.rem(partner[0] + lax.axis_index("lon") * cols, cols * n_lon)
    centre_col = centre % cols
    is_top = (lax.axis_index("lat") == n_lat - 1).astype(jnp.int32)
    kind = (centre_col >= cols // 2).astype(jnp.int32)
    where = jnp.stack([is_top, centre_col, kind])
    moves = Moves(n_lat, n_lon, centre // cols)

    own, west, east, part = scatter(where, arrived, bottom_level, diffusivity, channels, padded)
    west, east = moves.east(east), moves.west(west)
    part = moves.fold(kind, lambda fold, x: fold(x), part)
    top, low = slabs(own, west, east)

    def send(fold, top, low):
        return moves.north(top), moves.south(low), fold(top)

    around = (west, east, *moves.fold(1 - kind, send, top, low), part)
    fine, field = sweeps(where, own, around, length_scale, sigma, channels)
    local_fit, diffused = gather(fine, field, arrived, channels)
    returned = exchange(local_fit, owners)
    obs_fit = pl.pallas_call(
        unpack_kernel,
        out_shape=jax.ShapeDtypeStruct((channels, owners, slots), jnp.float32),
        in_specs=[vmem],
        out_specs=vmem,
        compiler_params=params(),
        name="unpack",
    )(returned)
    return obs_fit[None], diffused


def solution(mesh):
    return jax.shard_map(
        per_device,
        mesh=mesh,
        in_specs=(
            P(("lat", "lon"), None, None, None),
            P(("lat", "lon"), None, None),
            P(("lat", "lon"), None),
            P("lat", "lon"),
            P(None, "lat", "lon"),
            P("lon"),
            P(),
            P(),
        ),
        out_specs=(P(("lat", "lon"), None, None, None), P(None, "lat", "lon")),
        check_vma=False,
    )
```

```python
import functools

import jax
import jax.numpy as jnp
from jax import lax
from jax.experimental import pallas as pl
from jax.experimental.pallas import tpu as pltpu
from jax.sharding import PartitionSpec as P

LEV = 10
STEPS = 2
SWEEPS = 6
DEPTH = STEPS * SWEEPS
LANES = 128
SUB = 8
PER = LANES // DEPTH
MARGIN = -(-DEPTH // SUB) * SUB
COEFS = 3
MEGA = 1024 * 1024


def params(limit=8):
    return pltpu.CompilerParams(vmem_limit_bytes=limit * MEGA)


def lane_iota(shape):
    return lax.broadcasted_iota(jnp.int32, shape, len(shape) - 1)


def roll_lanes(x, shift):
    shift = shift % LANES
    return x if shift == 0 else pltpu.roll(x, shift, x.ndim - 1)


def pack_kernel(channels, width, cols, count_ref, value_ref, cell_ref, out_ref):
    owners, slots = cell_ref.shape
    for c in range(channels):
        out_ref[pl.ds(c, owners, stride=width), :] = value_ref[pl.ds(c * owners, owners), :]
    shape = (owners, owners)
    on_diagonal = lax.broadcasted_iota(jnp.int32, shape, 0) == lane_iota(shape)
    count = jnp.broadcast_to(count_ref[...].astype(jnp.float32), shape)
    count = jnp.sum(jnp.where(on_diagonal, count, 0.0), axis=1, keepdims=True)
    cell = cell_ref[...].astype(jnp.float32)
    row = jnp.floor((cell + 0.5) * (1.0 / cols))
    col = cell - row * cols
    row = jnp.where(lane_iota((owners, slots)).astype(jnp.float32) < count, row, -1.0)
    out_ref[pl.ds(channels, owners, stride=width), :] = row
    out_ref[pl.ds(channels + 1, owners, stride=width), :] = col


def unpack_kernel(in_ref, out_ref):
    channels, owners, _ = out_ref.shape
    for c in range(channels):
        out_ref[c] = in_ref[pl.ds(c, owners, stride=channels), :]


def exchange(x, owners):
    rows, slots = x.shape
    x = x.reshape(owners, 1, rows // owners * slots)
    x = lax.all_to_all(x, ("lat", "lon"), split_axis=0, concat_axis=0, tiled=True)
    return x.reshape(rows, slots)


def layout(cols, groups):
    window = cols + 2 * DEPTH
    phases = -(-window // (LANES // groups))
    return phases, -(-window // phases), -(-phases // groups)


def split(x):
    high = x.astype(jnp.bfloat16)
    low = (x - high.astype(jnp.float32)).astype(jnp.bfloat16)
    return high, low


def turned_window(cols, groups, group, n):
    phases, part, _ = layout(cols, groups)
    block = n // LANES
    lane = lax.rem(n - block * LANES + (LANES - group * part % LANES), LANES)
    i = lane // part
    phase = block * groups + i
    return jnp.where((i < groups) & (phase < phases), (lane - i * part) * phases + phase, -1)


def window_source(cols, w):
    at = jnp.where(w < DEPTH, w + cols, jnp.where(w < DEPTH + cols, w - DEPTH, w))
    return jnp.where((w >= 0) & (w < cols + 2 * DEPTH), at, -1)


def moved(x, matrix, exact=False):
    dot = functools.partial(jnp.dot, preferred_element_type=jnp.float32)
    high, low = split(x)
    parts = [high, low]
    if exact:
        rest = (x - high.astype(jnp.float32)) - low.astype(jnp.float32)
        parts.append(rest.astype(jnp.bfloat16))
    return dot(jnp.concatenate(parts, axis=1), jnp.concatenate([matrix] * len(parts), axis=0))


def part_starts(cols):
    return DEPTH, cols - DEPTH - LANES


def mirror_source(cols, centre_col, kind, w):
    column = centre_col + DEPTH - w
    left, right = part_starts(cols)
    in_part = jnp.where(kind == 0, column - left, column + cols - right)
    in_whole = jnp.where(kind == 0, column + cols, column)
    at_whole = jnp.where(in_whole < 0, cols + DEPTH + in_whole, in_whole + jnp.where(in_whole < cols, 0, DEPTH))
    from_whole = (in_whole >= -DEPTH) & (in_whole < cols + DEPTH)
    at = jnp.where(from_whole, at_whole, cols + LANES + in_part)
    return jnp.where((w >= 0) & (w < cols + 2 * DEPTH), at, -1)


def fill_tables(cols, where_ref, phase_ref, plain_ref, mirror_ref):
    is_top, centre_col, kind = where_ref[0], where_ref[1], where_ref[2]
    groups = phase_ref.shape[0]
    phases, part, _ = layout(cols, groups)

    def lanes_of(ref):
        return lax.broadcasted_iota(jnp.int32, (1, ref.shape[-1]), 1)

    def hot(ref, at):
        source = lax.broadcasted_iota(jnp.int32, ref.shape[-2:], 0)
        return jnp.where(source == at, 1.0, 0.0).astype(jnp.bfloat16)

    for g in range(groups):
        w = turned_window(cols, groups, g, lanes_of(phase_ref))
        phase_ref[g] = hot(phase_ref, window_source(cols, w))
        w = lanes_of(plain_ref) + DEPTH
        phase, lane = w % phases, w // phases
        at = ((phase % groups + g) * part + lane) % LANES
        plain_ref[g] = hot(plain_ref, phase // groups * LANES + at)

    @pl.when(is_top == 1)
    def _():
        for g in range(groups):
            w = turned_window(cols, groups, g, lanes_of(mirror_ref))
            mirror_ref[g] = hot(mirror_ref, mirror_source(cols, centre_col, kind, w))


def strip_count(rows, width=DEPTH):
    return -(-rows // (LANES // width))


def pack_strip(read, count, first, out_ref):
    for v in range(out_ref.shape[0]):
        total = None
        for s in range(min(PER, count - v * PER)):
            x = roll_lanes(read(v * PER + s), s * DEPTH - first)
            total = x if total is None else jnp.where(lane_iota(x.shape) >= s * DEPTH, x, total)
        out_ref[v] = total


def halo_lanes(west, at_west, east, at_east, at=0):
    split_at = lane_iota(west.shape) < at + DEPTH
    return jnp.where(split_at, roll_lanes(west, at - at_west), roll_lanes(east, at + DEPTH - at_east))


def slab_kernel(own_ref, west_ref, east_ref, top_ref, low_ref):
    rows, _, cols = own_ref.shape
    tiles, per = cols // LANES, PER // 2
    for ref, first in ((top_ref, rows - DEPTH), (low_ref, 0)):
        for m in range(tiles):
            ref[m * DEPTH : (m + 1) * DEPTH] = own_ref[first : first + DEPTH, :, m * LANES : (m + 1) * LANES]
        for v in range(ref.shape[0] - tiles * DEPTH):
            total = None
            for s in range(min(per, DEPTH - v * per)):
                i, at = divmod(first + v * per + s, PER)
                x = halo_lanes(west_ref[i], at * DEPTH, east_ref[i], at * DEPTH, s * 2 * DEPTH)
                total = x if s == 0 else jnp.where(lane_iota(x.shape) >= s * 2 * DEPTH, x, total)
            ref[tiles * DEPTH + v] = total


def slabs(own, west, east):
    _, width, cols = own.shape
    count = cols // LANES * DEPTH + strip_count(DEPTH, 2 * DEPTH)
    vmem = pl.BlockSpec(memory_space=pltpu.VMEM)
    return pl.pallas_call(
        slab_kernel,
        out_shape=(jax.ShapeDtypeStruct((count, width, LANES), jnp.float32),) * 2,
        in_specs=[vmem] * 3,
        out_specs=(vmem,) * 2,
        compiler_params=params(),
        name="slabs",
    )(own, west, east)


class Moves:
    def __init__(self, n_lat, n_lon, centre_tile):
        self.to_east = [(i, (i + 1) % n_lon) for i in range(n_lon)]
        self.to_west = [(b, a) for a, b in self.to_east]
        self.to_north = [(i, i + 1) for i in range(n_lat - 1)]
        self.to_south = [(b, a) for a, b in self.to_north]
        self.n_lon = n_lon
        self.first = (n_lat - 1) * n_lon
        self.centre_tile = centre_tile

    def east(self, x):
        return lax.ppermute(x, "lon", self.to_east)

    def west(self, x):
        return lax.ppermute(x, "lon", self.to_west)

    def north(self, x):
        return lax.ppermute(x, "lat", self.to_north)

    def south(self, x):
        return lax.ppermute(x, "lat", self.to_south)

    def fold(self, first_part, kind, send, *operands):
        first, n = self.first, self.n_lon

        def branch(tile, kind):
            pairs = [(first + s, first + (tile - first_part(kind) - s) % n) for s in range(n)]
            return lambda *xs: send(lambda x: lax.ppermute(x, ("lat", "lon"), pairs), kind, *xs)

        branches = [branch(t, k) for t in range(n) for k in (0, 1)]
        return lax.switch(self.centre_tile * 2 + kind, branches, *operands)


def scatter_kernel(channels, chunk, obs_ref, bottom_ref, kappa_ref, *refs):
    own_ref, west_ref, east_ref = refs[:3]
    part_refs, (left_ref, right_ref, sum_ref, blocks_ref) = refs[3:5], refs[5:]
    rows, padded, cols = own_ref.shape
    slots = obs_ref.shape[1]
    senders = blocks_ref.shape[0] // padded
    for c in range(channels + 2):
        blocks_ref[pl.ds(c, senders, stride=padded), :] = obs_ref[pl.ds(c, senders, stride=channels + 2), :]
    row_iota = lax.broadcasted_iota(jnp.int32, (rows, slots), 0).astype(jnp.float32)
    col_iota = lax.broadcasted_iota(jnp.int32, (cols, slots), 0).astype(jnp.float32)

    def body(step, carry):
        for s in range(chunk):
            at = pl.multiple_of((step * chunk + s) * padded, SUB)
            x = blocks_ref[pl.ds(at, padded), :]
            high, low = split(x)
            on_row = (row_iota == x[channels : channels + 1, :]).astype(jnp.bfloat16)
            on_col = (col_iota == x[channels + 1 : channels + 2, :]).astype(jnp.bfloat16)
            at = slice(s * slots, (s + 1) * slots)
            right_ref[:, at] = on_col
            for c in range(channels):
                left_ref[c * rows : (c + 1) * rows, at] = on_row * high[c : c + 1, :]
                left_ref[(channels + c) * rows : (channels + c + 1) * rows, at] = on_row * low[c : c + 1, :]
        part = lax.dot_general(
            left_ref[...], right_ref[...], (((1,), (1,)), ((), ())), preferred_element_type=jnp.float32
        )
        for m in range(cols // LANES):
            piece = part[:, m * LANES : (m + 1) * LANES]
            piece = piece[: channels * rows] + piece[channels * rows :]

            @pl.when(step == 0)
            def _():
                sum_ref[m, : channels * rows] = piece

            @pl.when(step > 0)
            def _():
                sum_ref[m, : channels * rows] += piece

        return carry

    lax.fori_loop(0, senders // chunk, body, 0)
    coefs = [bottom_ref[...].astype(jnp.float32), kappa_ref[0], kappa_ref[1]]
    for m in range(cols // LANES):
        at = slice(m * LANES, (m + 1) * LANES)
        for i, coef in enumerate(coefs):
            sum_ref[m, (channels + i) * rows : (channels + i + 1) * rows] = coef[:, at]
        for g in range(padded // SUB):
            for j in range(rows):
                own_ref[j, g * SUB : (g + 1) * SUB, at] = sum_ref[
                    m, pl.ds(g * SUB * rows + j, SUB, stride=rows), :
                ]
    pack_strip(lambda j: own_ref[j, :, :LANES], rows, 0, west_ref)
    pack_strip(lambda j: own_ref[j, :, cols - LANES :], rows, LANES - DEPTH, east_ref)
    for ref, start in zip(part_refs, part_starts(cols)):
        m, shift = divmod(start, LANES)
        for j in range(DEPTH):
            x = own_ref[rows - DEPTH + j, :, m * LANES : (m + 1) * LANES]
            y = own_ref[rows - DEPTH + j, :, (m + 1) * LANES : (m + 2) * LANES]
            here = lane_iota(x.shape) < LANES - shift
            ref[j] = jnp.where(here, roll_lanes(x, -shift), roll_lanes(y, -shift))


def scatter(obs, bottom_level, diffusivity, channels, padded):
    slots = obs.shape[1]
    senders = obs.shape[0] // (channels + 2)
    rows, cols = bottom_level.shape
    tiles = cols // LANES
    chunk = 16 if senders % 16 == 0 else 1
    vmem = pl.BlockSpec(memory_space=pltpu.VMEM)
    side = (strip_count(rows), padded, LANES)
    part = (DEPTH, padded, LANES)
    shapes = [(rows, padded, cols), side, side, part, part]
    shapes = [jax.ShapeDtypeStruct(shape, jnp.float32) for shape in shapes]
    return pl.pallas_call(
        functools.partial(scatter_kernel, channels, chunk),
        out_shape=tuple(shapes),
        in_specs=[vmem] * 3,
        out_specs=(vmem,) * len(shapes),
        scratch_shapes=[
            pltpu.VMEM((2 * channels * rows, chunk * slots), jnp.bfloat16),
            pltpu.VMEM((cols, chunk * slots), jnp.bfloat16),
            pltpu.VMEM((tiles, padded * rows, LANES), jnp.float32),
            pltpu.VMEM((senders * padded, slots), jnp.float32),
        ],
        compiler_params=params(28),
        cost_estimate=pl.CostEstimate(
            flops=4 * senders * slots * padded * rows * cols, bytes_accessed=0, transcendentals=0
        ),
        name="scatter",
    )(obs, bottom_level, diffusivity)


def east_of(xs, m):
    return xs[m + 1] if m + 1 < len(xs) else roll_lanes(xs[0], -1)


def west_of(xs, m):
    return xs[m - 1] if m > 0 else roll_lanes(xs[-1], 1)


def slab_row(ref, j, cols):
    tiles, per = cols // LANES, PER // 2
    side = roll_lanes(ref[tiles * DEPTH + j // per], -(j % per) * 2 * DEPTH)
    side = jnp.where(lane_iota(side.shape) < 2 * DEPTH, side, 0.0)
    return [ref[m * DEPTH + j] for m in range(tiles)] + [side]


def part_of_lane(first, part, shape):
    return lax.rem(lane_iota(shape) + (LANES - first % LANES), LANES) // part


def cell_terms(coef_at, part, wide_ref, coef_ref, cell_ref):
    groups = wide_ref.shape[0]
    _, count, total, _ = cell_ref.shape
    which = part_of_lane(0, part, (total, LANES))
    for i in range(COEFS):
        for m in range(count):
            block, turn = divmod(m, groups)
            x = wide_ref[groups - 1, block, pl.ds(coef_at + i, total, stride=SUB), :]
            first = (groups - 1 + turn) * part
            out = jnp.zeros_like(x)
            for g in range(groups):
                out = jnp.where(which == g, roll_lanes(x, g * part - first), out)
            coef_ref[i, m, :total] = out
            coef_ref[i, m, total:] = jnp.zeros((SUB, LANES), jnp.float32)
    bottom = [coef_ref[0, m, :total] for m in range(count)]
    lon = [coef_ref[1, m, :total] for m in range(count)]
    for m in range(count):
        cell_ref[0, m] = bottom[m]
        cell_ref[1, m] = jnp.minimum(bottom[m], east_of(bottom, m))
        cell_ref[2, m] = 0.5 * (lon[m] + east_of(lon, m))
        cell_ref[3, m] = jnp.minimum(bottom[m], coef_ref[0, m, 1 : total + 1])
        cell_ref[4, m] = 0.5 * (coef_ref[2, m, :total] + coef_ref[2, m, 1 : total + 1])


def gathered_phases(wide_ref, j, count, part):
    groups = wide_ref.shape[0]
    at = slice(j * SUB, (j + 1) * SUB)
    out = []
    for m in range(count):
        block, i = divmod(m, groups)
        which = part_of_lane(i * part, part, (SUB, LANES))
        x = wide_ref[groups - 1, block, at, :]
        for g in range(groups - 1):
            x = jnp.where(which == g, wide_ref[g, block, at, :], x)
        out.append(roll_lanes(x, -i * part))
    return out


def scattered_phases(xs, groups, part):
    out = [[] for _ in range(groups)]
    for first in range(0, len(xs), groups):
        turned = [roll_lanes(x, i * part) for i, x in enumerate(xs[first : first + groups])]
        for g in range(groups):
            which = part_of_lane(g * part, part, (SUB, LANES))
            x = turned[0]
            for i in range(1, len(turned)):
                x = jnp.where(which == i, turned[i], x)
            out[g].append(x)
    return out


def make_weights(part, level, scale, sigma, cell_ref, wide_ref, be_ref, bn_ref, root_ref, source_ref, state_ref):
    total, count = be_ref.shape[:2]
    zero = jnp.zeros((SUB, LANES), jnp.float32)
    below, root_below = [zero] * count, [zero] * count
    skip = MARGIN - DEPTH
    for j in range(skip, total - skip):

        def spread(i, m):
            return jnp.broadcast_to(cell_ref[i, m, j : j + 1, :], (SUB, LANES))

        a_e = [jnp.where(level < spread(1, m), scale * spread(2, m), 0.0) for m in range(count)]
        a_n = [jnp.where(level < spread(3, m), scale * spread(4, m), 0.0) for m in range(count)]
        start = gathered_phases(wide_ref, j, count, part)
        root = []
        for m in range(count):
            d = 1.0 + a_e[m] + west_of(a_e, m) + a_n[m] + below[m]
            x = lax.rsqrt(d)
            x = x * (1.5 - 0.5 * d * x * x)
            root.append(x)
            root_ref[j, m] = x
            state = start[m] * jnp.where(level < spread(0, m), sigma * (d * x), 0.0)
            state_ref[j, m] = state
            source_ref[j, m] = state * (x * x)
        for m in range(count):
            be_ref[j, m] = a_e[m] * root[m] * east_of(root, m)
            bn_ref[j - 1, m] = below[m] * root_below[m] * root[m]
        below, root_below = a_n, root


def run_sweeps(first, last, count, be_ref, bn_ref, source_ref, state_ref):
    every = range(be_ref.shape[1])

    def sweep(_, carry):
        here = [state_ref[first, m] for m in every]
        south = [bn_ref[first - 1, m] * state_ref[first - 1, m] for m in every]
        for j in range(first, last):
            north = [state_ref[j + 1, m] for m in every]
            to_e = [be_ref[j, m] for m in every]
            to_n = [bn_ref[j, m] for m in every]
            flow = [to_e[m] * here[m] for m in every]
            for m in every:
                new = source_ref[j, m] + south[m] + to_n[m] * north[m]
                state_ref[j, m] = new + (to_e[m] * east_of(here, m) + west_of(flow, m))
            south = [to_n[m] * here[m] for m in every]
            here = north
        return carry

    lax.fori_loop(0, count, sweep, 0)


def sweep_kernel(coef_at, where_ref, scale_ref, sigma_ref, *refs):
    own_ref, west_ref, east_ref = refs[:3]
    fine_ref, out_ref, window_ref, ghost_ref, wide_ref, coef_ref, cell_ref = refs[7:14]
    be_ref, bn_ref, root_ref, source_ref, state_ref, turn_ref = refs[14:20]
    phase_ref, plain_ref, mirror_ref = refs[20:23]
    south_ref, north_ref, whole_ref, part_ref = refs[23:27]
    copies = [
        pltpu.make_async_copy(source, target, refs[27].at[i])
        for i, (source, target) in enumerate(zip(refs[3:7], refs[23:27]))
    ]
    for copy in copies:
        copy.start()
    rows, padded, cols = own_ref.shape
    tiles, groups = cols // LANES, padded // SUB
    total, count = be_ref.shape[:2]
    part = layout(cols, groups)[1]
    body = MARGIN + rows
    skip = MARGIN - DEPTH
    is_top = where_ref[0]
    fill_tables(cols, where_ref, phase_ref, plain_ref, mirror_ref)

    def put(ref, j, pieces):
        for m, piece in enumerate(pieces):
            for g in range(groups):
                ref[g, m, j * SUB : (j + 1) * SUB] = piece[g * SUB : (g + 1) * SUB]

    def clear(ref, first, last):
        for j in range(first, last):
            put(ref, j, [jnp.zeros((padded, LANES), jnp.float32)] * ref.shape[1])

    clear(window_ref, 0, skip)
    lane = lane_iota((padded, LANES))
    for j in range(rows):
        v, s = divmod(j, PER)
        side = halo_lanes(west_ref[v], s * DEPTH, east_ref[v], s * DEPTH)
        side = jnp.where(lane < 2 * DEPTH, side, 0.0)
        put(
            window_ref,
            MARGIN + j,
            [own_ref[j, :, m * LANES : (m + 1) * LANES] for m in range(tiles)] + [side],
        )
    clear(ghost_ref, DEPTH, MARGIN)
    for copy in copies:
        copy.wait()
    for j in range(DEPTH):
        put(window_ref, skip + j, slab_row(south_ref, j, cols))

    def widen(ref, used, matrix_ref, first):
        for g in range(groups):
            x = jnp.concatenate([ref[g, t] for t in range(used)], axis=1)
            wide = moved(x, matrix_ref[g], exact=g == groups - 1)
            for k in range(wide_ref.shape[1]):
                wide_ref[g, k, first : first + x.shape[0]] = wide[:, k * LANES : (k + 1) * LANES]

    @pl.when(is_top == 1)
    def _():
        for j in range(DEPTH):
            i = DEPTH - 1 - j
            put(ghost_ref, j, slab_row(whole_ref, i, cols) + [part_ref[i]])
        widen(ghost_ref, tiles + 2, mirror_ref, body * SUB)

    @pl.when(is_top == 0)
    def _():
        for j in range(DEPTH):
            put(ghost_ref, j, slab_row(north_ref, j, cols))
        widen(ghost_ref, tiles + 1, phase_ref, body * SUB)

    widen(window_ref, tiles + 1, phase_ref, 0)
    cell_terms(coef_at, part, wide_ref, coef_ref, cell_ref)

    c = lax.broadcasted_iota(jnp.int32, (SUB, LANES), 0) + lane_iota((SUB, LANES)) // part * SUB
    level = jnp.where(c < LEV, c, jnp.where(c < 2 * LEV, c - LEV, jnp.where(c == 2 * LEV, 0, LEV)))
    scale, sigma = (jnp.zeros((SUB, LANES), jnp.float32) for _ in range(2))
    for i in range(sigma_ref.shape[0]):
        scale = jnp.where(c == i, scale_ref[i], scale)
        sigma = jnp.where(c == i, sigma_ref[i], sigma)
    make_weights(
        part, level.astype(jnp.float32), scale, sigma, cell_ref, wide_ref, be_ref, bn_ref, root_ref, source_ref, state_ref
    )

    done = 0
    for step in range(STEPS):

        def make_source(j, carry):
            for m in range(count):
                root = root_ref[j, m]
                source_ref[j, m] = state_ref[j, m] * (root * root)
            return carry

        if step > 0:
            lax.fori_loop(skip + done, total - skip - done, make_source, 0, unroll=4)
        for some in (SWEEPS - SWEEPS // 2, SWEEPS // 2):
            if some > 0:
                run_sweeps(
                    skip + done + 1, total - skip - done - 1, some, be_ref, bn_ref, source_ref, state_ref
                )
            done += some

    for j in range(rows):
        at = MARGIN + j
        scaled = [state_ref[at, m] * (sigma * root_ref[at, m]) for m in range(count)]
        for g, pieces in enumerate(scattered_phases(scaled, groups, part)):
            for k, piece in enumerate(pieces):
                window_ref[g, k, j * SUB : (j + 1) * SUB] = piece
    for g in range(groups):
        x = jnp.concatenate(
            [window_ref[g, k, : rows * SUB] for k in range(wide_ref.shape[1])], axis=1
        )
        plain = moved(x, plain_ref[g]).reshape(rows, SUB, cols)
        fine_ref[:, g * SUB : (g + 1) * SUB, :] = plain
        for m in range(tiles):
            for j in range(rows):
                turn_ref[pl.ds(j, SUB, stride=rows), :] = plain[j, :, m * LANES : (m + 1) * LANES]
            for s in range(SUB):
                if g * SUB + s < out_ref.shape[0]:
                    out_ref[g * SUB + s, :, m * LANES : (m + 1) * LANES] = turn_ref[
                        s * rows : (s + 1) * rows, :
                    ]


def sweeps(where, own, around, length_scale, sigma, channels):
    rows, padded, cols = own.shape
    total = rows + 2 * MARGIN
    groups = padded // SUB
    count, _, blocks = layout(cols, groups)
    smem = pl.BlockSpec(memory_space=pltpu.SMEM)
    vmem = pl.BlockSpec(memory_space=pltpu.VMEM)
    somewhere = pl.BlockSpec(memory_space=pl.ANY)
    plane = pltpu.VMEM((total, count, SUB, LANES), jnp.float32)
    late = around[2:]
    tiles = max(cols // LANES + 1, blocks)
    return pl.pallas_call(
        functools.partial(sweep_kernel, channels % SUB),
        out_shape=(
            jax.ShapeDtypeStruct((rows, padded, cols), jnp.float32),
            jax.ShapeDtypeStruct((channels, rows, cols), jnp.float32),
        ),
        in_specs=[smem] * 3 + [vmem] * 3 + [somewhere] * len(late),
        out_specs=(vmem, vmem),
        scratch_shapes=[
            pltpu.VMEM((groups, tiles, (MARGIN + rows) * SUB, LANES), jnp.float32),
            pltpu.VMEM((groups, cols // LANES + 2, MARGIN * SUB, LANES), jnp.float32),
            pltpu.VMEM((groups, blocks, total * SUB, LANES), jnp.float32),
            pltpu.VMEM((COEFS, count, total + SUB, LANES), jnp.float32),
            pltpu.VMEM((5, count, total, LANES), jnp.float32),
        ]
        + [plane] * 5
        + [pltpu.VMEM((SUB * rows, LANES), jnp.float32)]
        + [
            pltpu.VMEM((groups, cols + LANES, blocks * LANES), jnp.bfloat16),
            pltpu.VMEM((groups, blocks * LANES, cols), jnp.bfloat16),
            pltpu.VMEM((groups, cols + 2 * LANES, blocks * LANES), jnp.bfloat16),
        ]
        + [pltpu.VMEM(x.shape, jnp.float32) for x in late]
        + [pltpu.SemaphoreType.DMA((len(late),))],
        compiler_params=params(28),
        name="sweeps",
    )(where, length_scale, sigma, own, *around)


def gather_kernel(channels, pair, fine_ref, field_ref, obs_ref, out_ref, field_out_ref, *scratch):
    left_ref, cells_ref, blocks_ref, done_ref = scratch
    copy = pltpu.make_async_copy(field_ref, field_out_ref, done_ref)
    copy.start()
    rows, padded, cols = fine_ref.shape
    slots = obs_ref.shape[1]
    senders = blocks_ref.shape[0] // padded
    for i in (0, 1):
        cells_ref[pl.ds(i, senders, stride=SUB), :] = obs_ref[
            pl.ds(channels + i, senders, stride=channels + 2), :
        ]
    high, low = split(fine_ref[...].reshape(rows * padded, cols))
    left_ref[:, :cols] = high
    left_ref[:, cols:] = low
    col_iota = lax.broadcasted_iota(jnp.int32, (cols, slots), 0).astype(jnp.float32)

    def body(step, carry):
        hots = []
        for s in range(pair):
            col = cells_ref[pl.ds(pl.multiple_of((step * pair + s) * SUB, SUB), SUB), :][1:2, :]
            hots.append((col_iota == col).astype(jnp.bfloat16))
        hot = jnp.concatenate(hots, axis=1)
        found = jnp.dot(
            left_ref[...], jnp.concatenate([hot, hot], axis=0), preferred_element_type=jnp.float32
        )
        for s in range(pair):
            row = cells_ref[pl.ds(pl.multiple_of((step * pair + s) * SUB, SUB), SUB), :][:1, :]
            row = jnp.broadcast_to(row, (SUB, slots))
            total = [jnp.zeros((SUB, slots), jnp.float32)] * (padded // SUB)
            for j in range(rows):
                here = row == float(j)
                for g in range(padded // SUB):
                    at = j * padded + g * SUB
                    piece = found[at : at + SUB, s * slots : (s + 1) * slots]
                    total[g] = jnp.where(here, piece, total[g])
            for g in range(padded // SUB):
                at = pl.multiple_of((step * pair + s) * padded + g * SUB, SUB)
                blocks_ref[pl.ds(at, SUB), :] = total[g]
        return carry

    lax.fori_loop(0, senders // pair, body, 0)
    for c in range(channels):
        out_ref[pl.ds(c, senders, stride=channels), :] = blocks_ref[pl.ds(c, senders, stride=padded), :]
    copy.wait()


def gather(fine, field, obs, channels):
    rows, padded, cols = fine.shape
    slots = obs.shape[1]
    senders = obs.shape[0] // (channels + 2)
    pair = 32 if senders % 32 == 0 else 1
    vmem = pl.BlockSpec(memory_space=pltpu.VMEM)
    return pl.pallas_call(
        functools.partial(gather_kernel, channels, pair),
        out_shape=(
            jax.ShapeDtypeStruct((senders * channels, slots), jnp.float32),
            jax.ShapeDtypeStruct(field.shape, jnp.float32),
        ),
        in_specs=[vmem] * 3,
        out_specs=(vmem, pl.BlockSpec(memory_space=pl.ANY)),
        scratch_shapes=[
            pltpu.VMEM((rows * padded, 2 * cols), jnp.bfloat16),
            pltpu.VMEM((senders * SUB, slots), jnp.float32),
            pltpu.VMEM((senders * padded, slots), jnp.float32),
            pltpu.SemaphoreType.DMA,
        ],
        compiler_params=params(44),
        name="gather",
    )(fine, field, obs)


def per_device(
    obs_value, obs_cell, obs_count, bottom_level, diffusivity, partner, length_scale, sigma
):
    _, channels, owners, slots = obs_value.shape
    rows, cols = bottom_level.shape
    n_lat, n_lon = lax.axis_size("lat"), lax.axis_size("lon")
    padded = -(-(channels + COEFS) // SUB) * SUB
    vmem = pl.BlockSpec(memory_space=pltpu.VMEM)

    outgoing = pl.pallas_call(
        functools.partial(pack_kernel, channels, channels + 2, cols),
        grid=(1,),
        out_shape=jax.ShapeDtypeStruct((owners * (channels + 2), slots), jnp.float32),
        in_specs=[
            pl.BlockSpec((1, owners), lambda i: (0, 0)),
            pl.BlockSpec((channels * owners, slots), lambda i: (0, 0)),
            pl.BlockSpec((owners, slots), lambda i: (0, 0)),
        ],
        out_specs=vmem,
        compiler_params=params(60),
        name="pack",
    )(obs_count, obs_value.reshape(channels * owners, slots), obs_cell[0])
    arrived = exchange(outgoing, owners)

    centre = lax.rem(partner[0] + lax.axis_index("lon") * cols, cols * n_lon)
    centre_col = centre % cols
    is_top = (lax.axis_index("lat") == n_lat - 1).astype(jnp.int32)
    kind = (centre_col >= cols // 2).astype(jnp.int32)
    where = jnp.stack([is_top, centre_col, kind])
    moves = Moves(n_lat, n_lon, centre // cols)

    own, west, east, *parts = scatter(arrived, bottom_level, diffusivity, channels, padded)
    west, east = moves.east(east), moves.west(west)
    part = moves.fold(lambda k: k, kind, lambda fold, k, *xs: fold(xs[k]), *parts)
    top, low = slabs(own, west, east)

    def send(fold, _, top, low):
        return moves.north(top), moves.south(low), fold(top)

    around = (west, east, *moves.fold(lambda k: 1 - k, kind, send, top, low), part)
    fine, field = sweeps(where, own, around, length_scale, sigma, channels)
    local_fit, diffused = gather(fine, field, arrived, channels)
    returned = exchange(local_fit, owners)
    obs_fit = pl.pallas_call(
        unpack_kernel,
        out_shape=jax.ShapeDtypeStruct((channels, owners, slots), jnp.float32),
        in_specs=[vmem],
        out_specs=vmem,
        compiler_params=params(),
        name="unpack",
    )(returned)
    return obs_fit[None], diffused


def solution(mesh):
    return jax.shard_map(
        per_device,
        mesh=mesh,
        in_specs=(
            P(("lat", "lon"), None, None, None),
            P(("lat", "lon"), None, None),
            P(("lat", "lon"), None),
            P("lat", "lon"),
            P(None, "lat", "lon"),
            P("lon"),
            P(),
            P(),
        ),
        out_specs=(P(("lat", "lon"), None, None, None), P(None, "lat", "lon")),
        check_vma=False,
    )
```
